512 devices in a mesh: dp: 16 (over y, x_hi), owner: 32 (over x_lo, z, core).
Axes of the slice: x: 4 (x_hi: 2, x_lo: 2; x = x_hi * 2 + x_lo), y: 8, z: 8, core: 2. Of those that a mesh axis runs over, the one named last changes fastest.
Arguments:
- features: bfloat16 [4096, 16384], P('dp', 'owner'), may hold values from -33 to 33
Outputs:
- inverse_blocks: float32 [32, 512, 512], P('owner', 'dp')
- preconditioned: float32 [4096, 12288], P('dp', 'owner')
The draws below stay inside these ranges and needn't reach their ends.
All inputs are finite; a program needn't handle non-finite values. Where the reference program divides by a largest or mean magnitude, that divisor is 1e-20 or more.
Results may differ from the reference program's by a relative error of at most 0.034.
Values may be sent and summed in bfloat16 or wider, within the bound.
A program may use at most 64 MiB of HBM per device.

```python
import jax
import jax.numpy as jnp
from jax import lax

D = 4096
FFW = 12288
BLK = 512
ITERS = 6
TOK_DEV = 256
TOKENS = 4096
NB = 32
N_DP = 16


def draw_features(key, part):
    key = jax.random.fold_in(key, 11)
    key_rows, key_cols, key_act, key_grad = jax.random.split(key, 4)
    row_scale = jnp.exp(jax.random.uniform(key_rows, (TOKENS, 1), jnp.float32, -1.15, 1.15))
    col_scale = jnp.exp(jax.random.uniform(key_cols, (1, D + FFW), jnp.float32, -2.0, 2.0))
    act_base = jnp.clip(jax.random.normal(key_act, (TOKENS, D), jnp.float32), -5.0, 5.0)
    grad_base = jnp.clip(jax.random.normal(key_grad, (TOKENS, FFW), jnp.float32), -5.0, 5.0)
    grad_mixed = 0.8 * grad_base + 0.6 * jnp.tile(act_base, (1, FFW // D))
    base = jnp.concatenate([act_base, grad_mixed], axis=1)
    return (0.2 * base * row_scale * col_scale).astype(jnp.bfloat16)


def setup_inputs(seed: int = 0) -> dict:
    splits = jax.random.split(jax.random.key(seed), 2)
    return {
        "features": draw_features(jax.random.fold_in(splits[1], 71), 0),
    }


DAMPING = 1e-3


def invert(block_rows):
    identity = jnp.eye(BLK, dtype=jnp.float32)
    covariance = jnp.dot(block_rows.T, block_rows, preferred_element_type=jnp.float32) / TOKENS + DAMPING * identity
    largest = jnp.max(jnp.sum(jnp.abs(covariance), axis=1))
    current = identity / largest
    for sweep_index in range(ITERS):
        product_term = jnp.dot(covariance, current, precision=lax.Precision.HIGHEST)
        current = 2.0 * current - jnp.dot(product_term, current, precision=lax.Precision.HIGHEST)
    whitened = jnp.dot(block_rows, current.astype(jnp.bfloat16), preferred_element_type=jnp.float32).astype(jnp.bfloat16)
    return current, whitened


def reference(features):
    stacked = jnp.moveaxis(features.reshape(TOKENS, NB, BLK), 1, 0)
    inverse_blocks, whitened = lax.map(invert, stacked)
    grouped = jnp.moveaxis(whitened, 0, 1).reshape(N_DP, TOK_DEV, D + FFW)

    def accumulate(running, group_rows):
        piece = jnp.dot(group_rows[:, :D].T, group_rows[:, D:], preferred_element_type=jnp.float32).astype(jnp.bfloat16)
        piece = lax.optimization_barrier(piece)
        return running + piece.astype(jnp.float32), None

    running, unused = lax.scan(accumulate, jnp.zeros((D, FFW), jnp.float32), grouped)
    return inverse_blocks, running / TOKENS
```

```python
import functools

import jax
import jax.numpy as jnp
from jax import lax
from jax.experimental import pallas as pl
from jax.experimental.pallas import tpu as pltpu
from jax.sharding import PartitionSpec as P

BLK = 512
ITERS = 6
DAMPING = 0.001
UNIT = 128
MESH = pl.DeviceIdType.MESH
F32 = jnp.float32
BF16 = jnp.bfloat16


def dot(a, b):
    return jnp.dot(a, b, preferred_element_type=F32)


def dot_tn(a, b):
    return lax.dot_general(a, b, (((0,), (0,)), ((), ())), preferred_element_type=F32)


def kernel(
    ny, nz, tokens,
    x_ref, inv_ref, out_ref,
    feat, act, cov, cov_low, cov_in, cross, cross_low, cross_in,
    err, iterate, inv_low, inv_act, right, part, landed,
    gather_send, gather_recv, chain_send, chain_recv, swap_send, swap_recv,
    inv_send, inv_recv, out_send, out_recv,
):
    dp = lax.axis_index("dp")
    owner = lax.axis_index("owner")
    y, xh = dp // 2, dp % 2
    xl, z, core = owner // (2 * nz), (owner // 2) % nz, owner % 2
    half = x_ref.shape[0] // 2
    acts = ny
    gather_steps = ny - 1

    def device(y_=y, xh_=xh, xl_=xl, z_=z, core_=core):
        return (y_ * 2 + xh_, xl_ * (2 * nz) + z_ * 2 + core_)

    up, down = device(y_=(y + 1) % ny), device(y_=(y + ny - 1) % ny)
    partner = device(xh_=1 - xh)
    z_next, z_prev = device(z_=(z + 1) % nz), device(z_=(z + nz - 1) % nz)
    flip, sibling = device(xl_=1 - xl), device(core_=1 - core)

    on_core = core == y % 2
    away = (z + nz - y // 2) % nz
    forth = nz // 2
    is_root = on_core & (away == 0) & (xl == 0)
    routes = (
        (on_core & (away < forth), z_next),
        (on_core & ((away == 0) | (away > forth + 1)), z_prev),
        (is_root, flip),
        (on_core, sibling),
    )
    depth = xl + jnp.where(away <= forth, away, nz - away)
    lag = depth + (depth + 1) // 2 + jnp.where(on_core, 0, 1)
    max_depth = 1 + forth
    max_lag = max_depth + (max_depth + 1) // 2 + 1

    is_grad = owner >= acts
    grad = owner - acts

    barrier = pltpu.get_barrier_semaphore()
    for other in (up, down, partner, z_next, z_prev, flip, sibling):
        pl.semaphore_signal(barrier, inc=1, device_id=other, device_id_type=MESH)
    first_source = acts + (3 * owner) // 4
    last_source = acts + (3 * owner + 2) // 4

    @pl.when(first_source != owner)
    def _():
        pl.semaphore_signal(barrier, inc=1, device_id=(dp, first_source), device_id_type=MESH)

    @pl.when((last_source != owner) & (last_source != first_source))
    def _():
        pl.semaphore_signal(barrier, inc=1, device_id=(dp, last_source), device_id_type=MESH)

    feat[0] = x_ref[pl.ds(0, half), :]
    feat[1] = x_ref[pl.ds(half, half), :]
    targets = ((4 * grad) // 3, (4 * grad + 3) // 3)
    peers = sum(jnp.where(is_grad & (target != owner), 1, 0) for target in targets)
    pl.semaphore_wait(barrier, 7 + peers)

    def gather_copy(way, step, source):
        return pltpu.make_async_remote_copy(
            src_ref=feat.at[source],
            dst_ref=feat.at[2 + 2 * step + way],
            send_sem=gather_send.at[way, step],
            recv_sem=gather_recv.at[way, step],
            device_id=(up, down)[way],
            device_id_type=MESH,
        )

    def gather_source(way, step):
        if step < 2:
            return step if way == 0 else 1 - step
        return 2 + 2 * (step - 2) + way

    for step in range(min(2, gather_steps)):
        for way in range(2):
            gather_copy(way, step, gather_source(way, step)).start()
    own = x_ref[...]
    cov[...] = dot_tn(own, own)
    cross[...] = jnp.zeros_like(cross)

    def chain_copy(route, buffer, slot):
        return pltpu.make_async_remote_copy(
            src_ref=buffer.at[slot],
            dst_ref=act.at[slot],
            send_sem=chain_send.at[route, slot],
            recv_sem=chain_recv.at[slot],
            device_id=routes[route][1],
            device_id_type=MESH,
        )

    def chain_forward(buffer, slot):
        for route, (taken, _) in enumerate(routes):
            @pl.when(taken)
            def _():
                chain_copy(route, buffer, slot).start()

    def chain_step(it):
        step = it - lag

        @pl.when((step >= 0) & (step < ny))
        def _():
            for side in range(2):
                slot = 2 * step + side

                @pl.when(is_root)
                def _():
                    chain_forward(feat, slot)

                @pl.when(jnp.logical_not(is_root))
                def _():
                    chain_copy(3, act, slot).wait_recv()
                    chain_forward(act, slot)

            @pl.when(is_grad)
            def _():
                left = act[pl.ds(2 * step, 2)].reshape(2 * half, BLK)
                this = feat[pl.ds(2 * step, 2)].reshape(2 * half, BLK)
                cross[...] += dot_tn(left, this)

    def gather_step(it, carry):
        @pl.when(it >= 1)
        def _():
            step = it - 1
            for way in range(2):
                gather_copy(way, step, 0).wait_recv()

                @pl.when(step + 2 < gather_steps)
                def _():
                    gather_copy(way, step + 2, 2 + 2 * step + way).start()

        chain_step(it)

        @pl.when(it >= 1)
        def _():
            this = feat[pl.ds(2 * it, 2)].reshape(2 * half, BLK)
            cov[...] += dot_tn(this, this)

        return carry

    lax.fori_loop(0, ny, gather_step, 0)

    cov_low[...] = cov[...].astype(BF16)

    def swap_copy(row):
        place = (pl.ds(row * UNIT, UNIT), pl.ds(0, (row + 1) * UNIT))
        return pltpu.make_async_remote_copy(
            src_ref=cov_low.at[place],
            dst_ref=cov_in.at[place],
            send_sem=swap_send.at[row],
            recv_sem=swap_recv.at[row],
            device_id=partner,
            device_id_type=MESH,
        )

    blocks = BLK // UNIT
    for row in range(blocks):
        swap_copy(row).start()

    def late_step(it, carry):
        chain_step(it)
        return carry

    lax.fori_loop(ny, ny + max_lag, late_step, 0)

    cross_copy = pltpu.make_async_remote_copy(
        src_ref=cross_low,
        dst_ref=cross_in,
        send_sem=swap_send.at[blocks],
        recv_sem=swap_recv.at[blocks],
        device_id=partner,
        device_id_type=MESH,
    )

    @pl.when(is_grad)
    def _():
        cross_low[...] = cross[...].astype(BF16)
        cross_copy.start()

    for row in range(blocks):
        swap_copy(row).wait_recv()
        rows = pl.ds(row * UNIT, UNIT)
        for col in range(row + 1):
            cols = pl.ds(col * UNIT, UNIT)
            tile = (cov[rows, cols] + cov_in[rows, cols].astype(F32)) * (1.0 / tokens)
            if col == row:
                i = lax.broadcasted_iota(jnp.int32, (UNIT, UNIT), 0)
                j = lax.broadcasted_iota(jnp.int32, (UNIT, UNIT), 1)
                tile = tile + jnp.where(i == j, DAMPING, 0.0)
            err[rows, cols] = tile
            if col < row:
                err[cols, rows] = tile.T
    bound = jnp.max(jnp.sum(jnp.abs(err[...]), axis=1, keepdims=True), axis=0, keepdims=True)
    scale = 1.0 / bound
    i = lax.broadcasted_iota(jnp.int32, (BLK, BLK), 0)
    j = lax.broadcasted_iota(jnp.int32, (BLK, BLK), 1)
    first = err[...] * scale
    iterate[...] = jnp.where(i == j, 2.0, 0.0) - first
    low = first.astype(BF16)
    err[...] = 2.0 * first - dot(low, low)

    def newton(last):
        e = err[...]
        low = e.astype(BF16)
        x = iterate[...]
        high = x.astype(BF16)
        rest = (x - high.astype(F32)).astype(BF16)
        iterate[...] = 2.0 * x - (dot(high, low) + dot(rest, low))
        if not last:
            err[...] = 2.0 * e - dot(low, low)

    def newton_step(k, carry):
        newton(False)
        return carry

    lax.fori_loop(1, ITERS - 1, newton_step, 0)
    newton(True)
    inverse = iterate[...] * scale
    iterate[...] = inverse
    inv_low[...] = inverse.astype(BF16)
    rows_out = inv_ref.shape[1]
    inv_ref[0] = iterate[pl.ds(pl.multiple_of(dp * rows_out, rows_out), rows_out), :]

    pieces = inv_act.shape[0]
    piece = inv_act.shape[1]

    def inv_copy(route, rooted, index):
        start = pl.multiple_of(xh * (pieces * piece) + index * piece, piece)
        return pltpu.make_async_remote_copy(
            src_ref=inv_low.at[pl.ds(start, piece)] if rooted else inv_act.at[index],
            dst_ref=inv_act.at[index],
            send_sem=inv_send.at[route, index],
            recv_sem=inv_recv.at[index],
            device_id=routes[route][1],
            device_id_type=MESH,
        )

    def inv_forward(rooted, index):
        for route, (taken, _) in enumerate(routes):
            @pl.when(taken)
            def _():
                inv_copy(route, rooted, index).start()

    def inv_step(index, carry):
        @pl.when(is_root)
        def _():
            inv_forward(True, index)

        @pl.when(jnp.logical_not(is_root))
        def _():
            inv_copy(3, False, index).wait_recv()
            inv_forward(False, index)

        return carry

    lax.fori_loop(0, pieces, inv_step, 0)

    def out_place(unit):
        column = 4 * grad + unit
        return column // 3, column % 3

    def out_copy(unit):
        target, slot = out_place(unit)
        return pltpu.make_async_remote_copy(
            src_ref=part.at[unit],
            dst_ref=landed.at[slot],
            send_sem=out_send.at[unit],
            recv_sem=out_recv.at[slot],
            device_id=(dp, target),
            device_id_type=MESH,
        )

    def out_local(unit):
        _, slot = out_place(unit)
        return pltpu.make_async_copy(part.at[unit], landed.at[slot], out_recv.at[slot])

    @pl.when(is_grad)
    def _():
        cross_copy.wait_recv()
        whole = (cross[...] + cross_in[...].astype(F32)).astype(BF16)
        right[...] = dot(whole, inv_low[...]).astype(BF16)
        left = inv_act[...].reshape(pieces * piece, BLK)
        for unit in range(4):
            block = dot(left, right[:, unit * UNIT:(unit + 1) * UNIT])
            part[unit] = block.astype(BF16)
            target, _ = out_place(unit)

            @pl.when(target != owner)
            def _():
                out_copy(unit).start()

            @pl.when(target == owner)
            def _():
                out_local(unit).start()

    for slot in range(3):
        pltpu.make_async_copy(part.at[0], landed.at[slot], out_recv.at[slot]).wait()
        out_ref[:, slot * UNIT:(slot + 1) * UNIT] = landed[slot].astype(F32) * (1.0 / tokens)

    def gather_left(step, carry):
        for way in range(2):
            gather_copy(way, step, 0).wait_send()
        return carry

    lax.fori_loop(0, gather_steps, gather_left, 0)
    for row in range(blocks):
        swap_copy(row).wait_send()

    def chain_left(slot, carry):
        for route, (taken, _) in enumerate(routes):
            @pl.when(taken)
            def _():
                chain_copy(route, act, slot).wait_send()
        return carry

    lax.fori_loop(0, 2 * ny, chain_left, 0)

    def inv_left(index, carry):
        for route, (taken, _) in enumerate(routes):
            @pl.when(taken)
            def _():
                inv_copy(route, False, index).wait_send()
        return carry

    lax.fori_loop(0, pieces, inv_left, 0)

    @pl.when(is_grad)
    def _():
        cross_copy.wait_send()
        for unit in range(4):
            target, _ = out_place(unit)

            @pl.when(target != owner)
            def _():
                out_copy(unit).wait_send()


def per_device(features):
    dp_size = lax.axis_size("dp")
    owner_size = lax.axis_size("owner")
    ny, nz = dp_size // 2, owner_size // 4
    rows = features.shape[0]
    half = rows // 2
    pieces = 4
    blocks = BLK // UNIT
    square = (BLK, BLK)
    dma = pltpu.SemaphoreType.DMA
    return pl.pallas_call(
        functools.partial(kernel, ny, nz, rows * dp_size),
        out_shape=(
            jax.ShapeDtypeStruct((1, BLK // dp_size, BLK), F32),
            jax.ShapeDtypeStruct((BLK // 2, 3 * UNIT), F32),
        ),
        in_specs=[pl.BlockSpec(memory_space=pltpu.VMEM)],
        out_specs=[pl.BlockSpec(memory_space=pltpu.VMEM)] * 2,
        scratch_shapes=[
            pltpu.VMEM((2 * ny, half, BLK), BF16),
            pltpu.VMEM((2 * ny, half, BLK), BF16),
            pltpu.VMEM(square, F32),
            pltpu.VMEM(square, BF16),
            pltpu.VMEM(square, BF16),
            pltpu.VMEM(square, F32),
            pltpu.VMEM(square, BF16),
            pltpu.VMEM(square, BF16),
            pltpu.VMEM(square, F32),
            pltpu.VMEM(square, F32),
            pltpu.VMEM(square, BF16),
            pltpu.VMEM((pieces, BLK // 2 // pieces, BLK), BF16),
            pltpu.VMEM(square, BF16),
            pltpu.VMEM((4, BLK // 2, UNIT), BF16),
            pltpu.VMEM((3, BLK // 2, UNIT), BF16),
            dma((2, ny - 1)),
            dma((2, ny - 1)),
            dma((4, 2 * ny)),
            dma((2 * ny,)),
            dma((blocks + 1,)),
            dma((blocks + 1,)),
            dma((4, pieces)),
            dma((pieces,)),
            dma((4,)),
            dma((3,)),
        ],
        compiler_params=pltpu.CompilerParams(
            collective_id=0, has_side_effects=True, vmem_limit_bytes=48 * 2**20
        ),
    )(features)


def solution(mesh):
    return jax.shard_map(
        per_device,
        mesh=mesh,
        in_specs=(P("dp", "owner"),),
        out_specs=(P("owner", "dp", None), P("dp", "owner")),
        check_vma=False,
    )
```

```python
import functools

import jax
import jax.numpy as jnp
from jax import lax
from jax.experimental import pallas as pl
from jax.experimental.pallas import tpu as pltpu
from jax.sharding import PartitionSpec as P

BLK = 512
ITERS = 6
DAMPING = 0.001
UNIT = 128
MESH = pl.DeviceIdType.MESH
F32 = jnp.float32
BF16 = jnp.bfloat16


def dot(a, b):
    return jnp.dot(a, b, preferred_element_type=F32)


def dot_tn(a, b):
    return lax.dot_general(a, b, (((0,), (0,)), ((), ())), preferred_element_type=F32)


def kernel(
    ny, nz, tokens,
    x_ref, inv_ref, out_ref,
    feat, act, cov, cov_low, cov_in, cross, cross_low, cross_in,
    err, iterate, few, few_low, inv_low, inv_act, right, part, landed,
    gather_send, gather_recv, scatter_send, scatter_recv, flip_send, flip_recv,
    ring_send, ring_recv, near_send, near_recv, swap_send, swap_recv,
    inv_send, inv_recv, inv_near_send, inv_near_recv, out_send, out_recv,
):
    dp = lax.axis_index("dp")
    owner = lax.axis_index("owner")
    y, xh = dp // 2, dp % 2
    xl, z, core = owner // (2 * nz), (owner // 2) % nz, owner % 2
    rows = x_ref.shape[0]
    half = rows // 2
    acts = ny
    chips = 2 * nz
    group = ny // 2
    strip = rows // chips
    blocks = BLK // UNIT

    def device(y_=y, xh_=xh, xl_=xl, z_=z, core_=core):
        return (y_ * 2 + xh_, xl_ * (2 * nz) + z_ * 2 + core_)

    up, down = device(y_=(y + 1) % ny), device(y_=(y + ny - 1) % ny)
    partner = device(xh_=1 - xh)
    z_next, z_prev = device(z_=(z + 1) % nz), device(z_=(z + nz - 1) % nz)
    flip, sibling = device(xl_=1 - xl), device(core_=1 - core)

    is_act = owner < acts
    is_grad = owner >= acts
    grad = owner - acts

    barrier = pltpu.get_barrier_semaphore()
    for other in (up, down, partner, z_next, z_prev, flip, sibling):
        pl.semaphore_signal(barrier, inc=1, device_id=other, device_id_type=MESH)
    for k in range(group):
        source = 2 * k + core

        @pl.when((source != y) | (owner != y))
        def _():
            pl.semaphore_signal(
                barrier, inc=1, device_id=(source * 2 + xh, y), device_id_type=MESH
            )

    first_source = acts + (3 * owner) // 4
    last_source = acts + (3 * owner + 2) // 4

    @pl.when(first_source != owner)
    def _():
        pl.semaphore_signal(barrier, inc=1, device_id=(dp, first_source), device_id_type=MESH)

    @pl.when((last_source != owner) & (last_source != first_source))
    def _():
        pl.semaphore_signal(barrier, inc=1, device_id=(dp, last_source), device_id_type=MESH)

    def place(source):
        return source % 2, ((source + ny - y) % ny) // 2

    own_par, own_k = place(y)
    feat[own_par, own_k] = x_ref[...]

    targets = ((4 * grad) // 3, (4 * grad + 3) // 3)
    peers = sum(jnp.where(is_grad & (target != owner), 1, 0) for target in targets)
    peers = peers + jnp.where(is_act, chips, 0) - jnp.where(owner == y, 1, 0)
    pl.semaphore_wait(barrier, 7 + peers)

    gather_steps = ny - 1

    def gather_place(way, step):
        away = step // 2 + 1
        source = (y + ny - away) % ny if way == 0 else (y + away) % ny
        part_ = step % 2 if way == 0 else 1 - step % 2
        return source, part_

    def gather_copy(way, step):
        source, part_ = gather_place(way, step)
        par, k = place(source)
        there = feat.at[par, k, pl.ds(part_ * half, half)]
        return pltpu.make_async_remote_copy(
            src_ref=there,
            dst_ref=there,
            send_sem=gather_send.at[way, step],
            recv_sem=gather_recv.at[way, step],
            device_id=(up, down)[way],
            device_id_type=MESH,
        )

    def gather_start(way, step):
        if step < 2:
            source, part_ = y, (step if way == 0 else 1 - step)
        else:
            source, part_ = gather_place(way, step - 2)
        par, k = place(source)
        target_y = (y + 1) % ny if way == 0 else (y + ny - 1) % ny
        target_k = ((source + ny - target_y) % ny) // 2
        pltpu.make_async_remote_copy(
            src_ref=feat.at[par, k, pl.ds(part_ * half, half)],
            dst_ref=feat.at[par, target_k, pl.ds(part_ * half, half)],
            send_sem=gather_send.at[way, step],
            recv_sem=gather_recv.at[way, step],
            device_id=(up, down)[way],
            device_id_type=MESH,
        ).start()

    for step in range(2):
        for way in range(2):
            gather_start(way, step)

    def scatter_copy(chip):
        k = ((y + ny - owner) % ny) // 2
        strip_rows = pl.ds(chip * strip, strip)
        return pltpu.make_async_remote_copy(
            src_ref=x_ref.at[strip_rows],
            dst_ref=act.at[y % 2, k, strip_rows],
            send_sem=scatter_send.at[chip],
            recv_sem=scatter_recv.at[k],
            device_id=(owner * 2 + xh, 2 * chip + y % 2),
            device_id_type=MESH,
        )

    def scatter_local(chip):
        k = ((y + ny - owner) % ny) // 2
        strip_rows = pl.ds(chip * strip, strip)
        return pltpu.make_async_copy(
            x_ref.at[strip_rows], act.at[y % 2, k, strip_rows], scatter_recv.at[k]
        )

    @pl.when(is_act)
    def _():
        for chip in range(chips):
            mine = (owner == y) & (owner // 2 == chip)

            @pl.when(mine)
            def _():
                scatter_local(chip).start()

            @pl.when(jnp.logical_not(mine))
            def _():
                scatter_copy(chip).start()

    own = x_ref[...]
    cov[...] = dot_tn(own, own)

    def strips(par, chip):
        return act.at[par, :, pl.ds(pl.multiple_of(chip * strip, strip), strip)]

    def strips_copy(chip, send_sem, recv_sem, target, par=core):
        return pltpu.make_async_remote_copy(
            src_ref=strips(par, chip),
            dst_ref=strips(par, chip),
            send_sem=send_sem,
            recv_sem=recv_sem,
            device_id=target,
            device_id_type=MESH,
        )

    my_chip = xl * nz + z
    flip_chip = (1 - xl) * nz + z

    def near_copy(index, chip):
        return strips_copy(chip, near_send.at[index], near_recv.at[index], sibling)

    def ring_place(way, step):
        away = step // 2 + 1
        source = (z + nz - away) % nz if way == 0 else (z + away) % nz
        return (step % 2 if way == 0 else 1 - step % 2) * nz + source

    def ring_copy(way, step, chip):
        return strips_copy(
            chip, ring_send.at[way, step], ring_recv.at[way, step], (z_next, z_prev)[way]
        )

    def scatter_done():
        for k in range(group):
            strip_rows = pl.ds(pl.multiple_of(my_chip * strip, strip), strip)
            pltpu.make_async_copy(
                x_ref.at[pl.ds(0, strip)], act.at[core, k, strip_rows], scatter_recv.at[k]
            ).wait()
        strips_copy(my_chip, flip_send, flip_recv, flip).start()
        for column in range(2):
            @pl.when(xl == column)
            def _():
                ring_copy(0, column, my_chip).start()
                ring_copy(1, 1 - column, my_chip).start()
        near_copy(0, my_chip).start()

    def flip_done():
        strips_copy(flip_chip, flip_send, flip_recv, flip).wait_recv()
        for column in range(2):
            @pl.when(xl == 1 - column)
            def _():
                ring_copy(0, column, flip_chip).start()
                ring_copy(1, 1 - column, flip_chip).start()
        near_copy(1, flip_chip).start()

    def ring_done(step):
        for way in range(2):
            chip = ring_place(way, step)
            ring_copy(way, step, chip).wait_recv()
            if step + 2 < nz - 1:
                ring_copy(way, step + 2, chip).start()
            near_copy(2 + 2 * step + way, chip).start()

    def gather_done(step):
        for way in range(2):
            gather_copy(way, step).wait_recv()
            if step + 2 < gather_steps:
                gather_start(way, step + 2)

    def add_cov(away):
        sources = [(y + away) % ny]
        if 2 * away < ny:
            sources.append((y + ny - away) % ny)
        for source in sources:
            par, k = place(source)
            this = feat[par, k]
            cov[...] += dot_tn(this, this)

    gather_done(0)
    gather_done(1)
    scatter_done()
    add_cov(1)
    gather_done(2)
    flip_done()
    gather_done(3)
    add_cov(2)
    ring_done(0)
    gather_done(4)
    ring_done(1)
    gather_done(5)
    ring_done(2)
    add_cov(3)
    ring_done(3)
    gather_done(6)
    add_cov(4)

    cov_low[...] = cov[...].astype(BF16)

    def swap_copy(row):
        tile = (pl.ds(row * UNIT, UNIT), pl.ds(0, (row + 1) * UNIT))
        return pltpu.make_async_remote_copy(
            src_ref=cov_low.at[tile],
            dst_ref=cov_in.at[tile],
            send_sem=swap_send.at[row],
            recv_sem=swap_recv.at[row],
            device_id=partner,
            device_id_type=MESH,
        )

    for row in range(blocks):
        swap_copy(row).start()

    for step in range(4, nz - 1):
        ring_done(step)
    for index in range(chips):
        if index == 0:
            chip = my_chip
        elif index == 1:
            chip = flip_chip
        else:
            chip = ring_place(index % 2, index // 2 - 1)
        strips_copy(
            chip, near_send.at[index], near_recv.at[index], sibling, par=1 - core
        ).wait_recv()

    cross_copy = pltpu.make_async_remote_copy(
        src_ref=cross_low,
        dst_ref=cross_in,
        send_sem=swap_send.at[blocks],
        recv_sem=swap_recv.at[blocks],
        device_id=partner,
        device_id_type=MESH,
    )

    @pl.when(is_grad)
    def _():
        cross[...] = dot_tn(act[...].reshape(ny * rows, BLK), feat[...].reshape(ny * rows, BLK))
        cross_low[...] = cross[...].astype(BF16)
        cross_copy.start()

    for row in range(blocks):
        swap_copy(row).wait_recv()
        tile_rows = pl.ds(row * UNIT, UNIT)
        for col in range(row + 1):
            tile_cols = pl.ds(col * UNIT, UNIT)
            tile = (cov[tile_rows, tile_cols] + cov_in[tile_rows, tile_cols].astype(F32)) * (
                1.0 / tokens
            )
            if col == row:
                i = lax.broadcasted_iota(jnp.int32, (UNIT, UNIT), 0)
                j = lax.broadcasted_iota(jnp.int32, (UNIT, UNIT), 1)
                tile = tile + jnp.where(i == j, DAMPING, 0.0)
            err[tile_rows, tile_cols] = tile
            if col < row:
                err[tile_cols, tile_rows] = tile.T
    bound = jnp.max(jnp.sum(jnp.abs(err[...]), axis=1, keepdims=True), axis=0, keepdims=True)
    scale = 1.0 / bound
    err[...] = err[...] * scale

    def first_iterate(ref, offset, count, start):
        start = pl.multiple_of(start, count) if not isinstance(start, int) else start
        i = lax.broadcasted_iota(jnp.int32, (count, BLK), 0) + start
        j = lax.broadcasted_iota(jnp.int32, (count, BLK), 1)
        ref[pl.ds(offset, count), :] = jnp.where(i == j, 2.0, 0.0) - err[pl.ds(start, count), :]

    def newton(ref, last):
        e = err[...]
        low = e.astype(BF16)
        x = ref[...]
        high = x.astype(BF16)
        rest = (x - high.astype(F32)).astype(BF16)
        ref[...] = 2.0 * x - (dot(high, low) + dot(rest, low))
        if not last:
            err[...] = 2.0 * e - dot(low, low)

    def iterations(ref):
        first = err[...]
        low = first.astype(BF16)
        err[...] = 2.0 * first - dot(low, low)

        def newton_step(k, carry):
            newton(ref, False)
            return carry

        lax.fori_loop(1, ITERS - 1, newton_step, 0)
        newton(ref, True)

    rows_out = inv_ref.shape[1]
    rows_sent = few_low.shape[0]
    out_start = pl.multiple_of(dp * rows_out, rows_out)
    first_piece = acts // 2

    def inv_copy(chip):
        return pltpu.make_async_remote_copy(
            src_ref=few_low,
            dst_ref=inv_act.at[y // 2, y % 2],
            send_sem=inv_send.at[chip],
            recv_sem=inv_recv.at[y // 2],
            device_id=(owner * 2 + xh, 2 * chip + y % 2),
            device_id_type=MESH,
        )

    @pl.when(is_act)
    def _():
        first_iterate(few, 0, rows_out, dp * rows_out)
        first_iterate(few, rows_out, rows_sent, xh * (BLK // 2) + y * rows_sent)
        iterations(few)
        few_low[...] = (few[pl.ds(rows_out, rows_sent), :] * scale).astype(BF16)
        for chip in range(first_piece, chips):
            inv_copy(chip).start()
        inv_ref[0] = few[pl.ds(0, rows_out), :] * scale

    def inv_near(k, par):
        return pltpu.make_async_remote_copy(
            src_ref=inv_act.at[k, par],
            dst_ref=inv_act.at[k, par],
            send_sem=inv_near_send.at[k],
            recv_sem=inv_near_recv.at[k],
            device_id=sibling,
            device_id_type=MESH,
        )

    def out_place(unit):
        column = 4 * grad + unit
        return column // 3, column % 3

    def out_copy(unit):
        target, slot = out_place(unit)
        return pltpu.make_async_remote_copy(
            src_ref=part.at[unit],
            dst_ref=landed.at[slot],
            send_sem=out_send.at[unit],
            recv_sem=out_recv.at[slot],
            device_id=(dp, target),
            device_id_type=MESH,
        )

    def out_local(unit):
        _, slot = out_place(unit)
        return pltpu.make_async_copy(part.at[unit], landed.at[slot], out_recv.at[slot])

    @pl.when(is_grad)
    def _():
        first_iterate(iterate, 0, BLK, 0)
        iterations(iterate)
        inverse = iterate[...] * scale
        iterate[...] = inverse
        inv_low[...] = inverse.astype(BF16)
        inv_ref[0] = iterate[pl.ds(out_start, rows_out), :]

        cross_copy.wait_recv()
        whole = (cross[...] + cross_in[...].astype(F32)).astype(BF16)
        right[...] = dot(whole, inv_low[...]).astype(BF16)
        for k in range(group):
            pltpu.make_async_copy(few_low, inv_act.at[k, core], inv_recv.at[k]).wait()
            inv_near(k, core).start()
        for k in range(group):
            inv_near(k, 1 - core).wait_recv()
        left = inv_act[...].reshape(BLK // 2, BLK)
        for unit in range(4):
            block = dot(left, right[:, unit * UNIT:(unit + 1) * UNIT])
            part[unit] = block.astype(BF16)
            target, _ = out_place(unit)

            @pl.when(target != owner)
            def _():
                out_copy(unit).start()

            @pl.when(target == owner)
            def _():
                out_local(unit).start()

    for slot in range(3):
        pltpu.make_async_copy(part.at[0], landed.at[slot], out_recv.at[slot]).wait()
        out_ref[:, slot * UNIT:(slot + 1) * UNIT] = landed[slot].astype(F32) * (1.0 / tokens)

    for step in range(gather_steps):
        for way in range(2):
            gather_copy(way, step).wait_send()
    for step in range(nz - 1):
        for way in range(2):
            ring_copy(way, step, my_chip).wait_send()
    strips_copy(my_chip, flip_send, flip_recv, flip).wait_send()
    for index in range(chips):
        near_copy(index, my_chip).wait_send()
    for row in range(blocks):
        swap_copy(row).wait_send()

    @pl.when(is_act)
    def _():
        for chip in range(chips):
            mine = (owner == y) & (owner // 2 == chip)

            @pl.when(jnp.logical_not(mine))
            def _():
                scatter_copy(chip).wait_send()
        for chip in range(first_piece, chips):
            inv_copy(chip).wait_send()

    @pl.when(is_grad)
    def _():
        cross_copy.wait_send()
        for k in range(group):
            inv_near(k, core).wait_send()
        for unit in range(4):
            target, _ = out_place(unit)

            @pl.when(target != owner)
            def _():
                out_copy(unit).wait_send()


def per_device(features):
    dp_size = lax.axis_size("dp")
    owner_size = lax.axis_size("owner")
    ny, nz = dp_size // 2, owner_size // 4
    chips = 2 * nz
    rows = features.shape[0]
    blocks = BLK // UNIT
    rows_out = BLK // dp_size
    square = (BLK, BLK)
    dma = pltpu.SemaphoreType.DMA
    return pl.pallas_call(
        functools.partial(kernel, ny, nz, rows * dp_size),
        out_shape=(
            jax.ShapeDtypeStruct((1, rows_out, BLK), F32),
            jax.ShapeDtypeStruct((BLK // 2, 3 * UNIT), F32),
        ),
        in_specs=[pl.BlockSpec(memory_space=pltpu.VMEM)],
        out_specs=[pl.BlockSpec(memory_space=pltpu.VMEM)] * 2,
        scratch_shapes=[
            pltpu.VMEM((2, ny // 2, rows, BLK), BF16),
            pltpu.VMEM((2, ny // 2, rows, BLK), BF16),
            pltpu.VMEM(square, F32),
            pltpu.VMEM(square, BF16),
            pltpu.VMEM(square, BF16),
            pltpu.VMEM(square, F32),
            pltpu.VMEM(square, BF16),
            pltpu.VMEM(square, BF16),
            pltpu.VMEM(square, F32),
            pltpu.VMEM(square, F32),
            pltpu.VMEM((2 * rows_out, BLK), F32),
            pltpu.VMEM((rows_out, BLK), BF16),
            pltpu.VMEM(square, BF16),
            pltpu.VMEM((ny // 2, 2, rows_out, BLK), BF16),
            pltpu.VMEM(square, BF16),
            pltpu.VMEM((4, BLK // 2, UNIT), BF16),
            pltpu.VMEM((3, BLK // 2, UNIT), BF16),
            dma((2, ny - 1)),
            dma((2, ny - 1)),
            dma((chips,)),
            dma((ny // 2,)),
            dma(()),
            dma(()),
            dma((2, nz - 1)),
            dma((2, nz - 1)),
            dma((chips,)),
            dma((chips,)),
            dma((blocks + 1,)),
            dma((blocks + 1,)),
            dma((chips,)),
            dma((ny // 2,)),
            dma((ny // 2,)),
            dma((ny // 2,)),
            dma((4,)),
            dma((3,)),
        ],
        compiler_params=pltpu.CompilerParams(
            collective_id=0, has_side_effects=True, vmem_limit_bytes=48 * 2**20
        ),
    )(features)


def solution(mesh):
    return jax.shard_map(
        per_device,
        mesh=mesh,
        in_specs=(P("dp", "owner"),),
        out_specs=(P("owner", "dp", None), P("dp", "owner")),
        check_vma=False,
    )
```

```python
import functools

import jax
import jax.numpy as jnp
from jax import lax
from jax.experimental import pallas as pl
from jax.experimental.pallas import tpu as pltpu
from jax.sharding import PartitionSpec as P

BLK = 512
ITERS = 6
DAMPING = 0.001
UNIT = 128
MESH = pl.DeviceIdType.MESH
F32 = jnp.float32
BF16 = jnp.bfloat16


def dot(a, b):
    return jnp.dot(a, b, preferred_element_type=F32)


def dot_tn(a, b):
    return lax.dot_general(a, b, (((0,), (0,)), ((), ())), preferred_element_type=F32)


def kernel(
    ny, nz, tokens,
    x_ref, inv_ref, out_ref,
    feat, act, cov, cov_low, cov_in, cross, cross_low, cross_in,
    err, iterate, few, inv_low, inv_act, right, part, landed,
    gather_send, gather_recv, chain_send, chain_recv, swap_send, swap_recv,
    inv_send, inv_recv, out_send, out_recv,
):
    dp = lax.axis_index("dp")
    owner = lax.axis_index("owner")
    y, xh = dp // 2, dp % 2
    xl, z, core = owner // (2 * nz), (owner // 2) % nz, owner % 2
    rows = x_ref.shape[0]
    quarter = rows // 4
    acts = ny
    gather_steps = (ny - 1) * 2

    def device(y_=y, xh_=xh, xl_=xl, z_=z, core_=core):
        return (y_ * 2 + xh_, xl_ * (2 * nz) + z_ * 2 + core_)

    up, down = device(y_=(y + 1) % ny), device(y_=(y + ny - 1) % ny)
    partner = device(xh_=1 - xh)
    sibling = device(core_=1 - core)

    is_grad = owner >= acts
    grad = owner - acts

    z_next, z_prev = device(z_=(z + 1) % nz), device(z_=(z + nz - 1) % nz)
    flip = device(xl_=1 - xl)
    on_core = core == y % 2
    away = (z + nz - y // 2) % nz
    forth = nz // 2
    is_root = on_core & (away == 0) & (xl == 0)
    has_parent = on_core & jnp.logical_not(is_root)
    parent = jnp.where(away == 0, flip[1], jnp.where(away <= forth, z_prev[1], z_next[1]))
    receives = has_parent | (jnp.logical_not(on_core) & is_grad)
    routes = [
        (on_core & (away < forth), z_next),
        (on_core & ((away == 0) | (away > forth + 1)), z_prev),
        (is_root, flip),
        (on_core & is_grad, sibling),
    ]
    depth = xl + jnp.where(away <= forth, away, nz - away)
    lag = depth + (depth + 1) // 2 + jnp.where(on_core, 0, 1)
    max_depth = 1 + forth
    max_lag = max_depth + (max_depth + 1) // 2 + 1

    barrier = pltpu.get_barrier_semaphore()
    for other in (up, down, partner):
        pl.semaphore_signal(barrier, inc=1, device_id=other, device_id_type=MESH)

    @pl.when(is_grad)
    def _():
        pl.semaphore_signal(barrier, inc=1, device_id=sibling, device_id_type=MESH)

    @pl.when(has_parent)
    def _():
        pl.semaphore_signal(
            barrier, inc=1, device_id=(dp, parent), device_id_type=MESH
        )

    first_source = acts + (3 * owner) // 4
    last_source = acts + (3 * owner + 2) // 4

    @pl.when(first_source != owner)
    def _():
        pl.semaphore_signal(barrier, inc=1, device_id=(dp, first_source), device_id_type=MESH)

    @pl.when((last_source != owner) & (last_source != first_source))
    def _():
        pl.semaphore_signal(barrier, inc=1, device_id=(dp, last_source), device_id_type=MESH)

    for index in range(4):
        feat[index] = x_ref[pl.ds(index * quarter, quarter), :]
    targets = ((4 * grad) // 3, (4 * grad + 3) // 3)
    peers = sum(jnp.where(is_grad & (target != owner), 1, 0) for target in targets)
    peers = peers + jnp.where(is_grad, 1, 0)
    for taken, _ in routes[:3]:
        peers = peers + jnp.where(taken, 1, 0)
    pl.semaphore_wait(barrier, 3 + peers)

    def gather_copy(way, step, source):
        return pltpu.make_async_remote_copy(
            src_ref=feat.at[source],
            dst_ref=feat.at[4 + 2 * step + way],
            send_sem=gather_send.at[way, step],
            recv_sem=gather_recv.at[way, step],
            device_id=(up, down)[way],
            device_id_type=MESH,
        )

    for step in range(4):
        for way in range(2):
            gather_copy(way, step, step if way == 0 else 3 - step).start()
    own = x_ref[...]
    cov[...] = dot_tn(own, own)
    cross[...] = jnp.zeros_like(cross)

    def chain_copy(route, buffer, slot):
        return pltpu.make_async_remote_copy(
            src_ref=buffer.at[pl.ds(2 * slot, 2)],
            dst_ref=act.at[pl.ds(2 * slot, 2)],
            send_sem=chain_send.at[route, slot],
            recv_sem=chain_recv.at[slot],
            device_id=routes[route][1],
            device_id_type=MESH,
        )

    def chain_forward(buffer, slot):
        for route, (taken, _) in enumerate(routes):
            @pl.when(taken)
            def _():
                chain_copy(route, buffer, slot).start()

    def chain_step(it):
        step = it - lag

        @pl.when((step >= 0) & (step < ny))
        def _():
            for side in range(2):
                slot = 2 * step + side

                @pl.when(is_root)
                def _():
                    chain_forward(feat, slot)

                @pl.when(receives)
                def _():
                    chain_copy(3, act, slot).wait_recv()
                    chain_forward(act, slot)

            @pl.when(is_grad)
            def _():
                left = act[pl.ds(4 * step, 4)].reshape(rows, BLK)
                this = feat[pl.ds(4 * step, 4)].reshape(rows, BLK)
                cross[...] += dot_tn(left, this)

    def gather_step(it, carry):
        @pl.when(it >= 1)
        def _():
            for half in range(2):
                step = 2 * (it - 1) + half
                for way in range(2):
                    gather_copy(way, step, 0).wait_recv()

                    @pl.when(step + 4 < gather_steps)
                    def _():
                        gather_copy(way, step + 4, 4 + 2 * step + way).start()

        chain_step(it)

        @pl.when(it >= 1)
        def _():
            this = feat[pl.ds(4 * it, 4)].reshape(rows, BLK)
            cov[...] += dot_tn(this, this)

        return carry

    lax.fori_loop(0, ny, gather_step, 0)

    cov_low[...] = cov[...].astype(BF16)

    def swap_copy(row):
        place = (pl.ds(row * UNIT, UNIT), pl.ds(0, (row + 1) * UNIT))
        return pltpu.make_async_remote_copy(
            src_ref=cov_low.at[place],
            dst_ref=cov_in.at[place],
            send_sem=swap_send.at[row],
            recv_sem=swap_recv.at[row],
            device_id=partner,
            device_id_type=MESH,
        )

    blocks = BLK // UNIT
    for row in range(blocks):
        swap_copy(row).start()

    def late_step(it, carry):
        chain_step(it)
        return carry

    lax.fori_loop(ny, ny + max_lag, late_step, 0)

    cross_copy = pltpu.make_async_remote_copy(
        src_ref=cross_low,
        dst_ref=cross_in,
        send_sem=swap_send.at[blocks],
        recv_sem=swap_recv.at[blocks],
        device_id=partner,
        device_id_type=MESH,
    )

    @pl.when(is_grad)
    def _():
        cross_low[...] = cross[...].astype(BF16)
        cross_copy.start()

    for row in range(blocks):
        swap_copy(row).wait_recv()
        rows = pl.ds(row * UNIT, UNIT)
        for col in range(row + 1):
            cols = pl.ds(col * UNIT, UNIT)
            tile = (cov[rows, cols] + cov_in[rows, cols].astype(F32)) * (1.0 / tokens)
            if col == row:
                i = lax.broadcasted_iota(jnp.int32, (UNIT, UNIT), 0)
                j = lax.broadcasted_iota(jnp.int32, (UNIT, UNIT), 1)
                tile = tile + jnp.where(i == j, DAMPING, 0.0)
            err[rows, cols] = tile
            if col < row:
                err[cols, rows] = tile.T
    bound = jnp.max(jnp.sum(jnp.abs(err[...]), axis=1, keepdims=True), axis=0, keepdims=True)
    scale = 1.0 / bound
    first = err[...] * scale
    err[...] = first

    def first_iterate(ref, offset, count, start):
        i = lax.broadcasted_iota(jnp.int32, (count, BLK), 0) + start
        j = lax.broadcasted_iota(jnp.int32, (count, BLK), 1)
        ref[pl.ds(offset, count), :] = jnp.where(i == j, 2.0, 0.0) - err[pl.ds(start, count), :]

    def newton(ref, last):
        e = err[...]
        low = e.astype(BF16)
        x = ref[...]
        high = x.astype(BF16)
        rest = (x - high.astype(F32)).astype(BF16)
        ref[...] = 2.0 * x - (dot(high, low) + dot(rest, low))
        if not last:
            err[...] = 2.0 * e - dot(low, low)

    def iterations(ref):
        e = err[...]
        low = e.astype(BF16)
        err[...] = 2.0 * e - dot(low, low)

        def newton_step(k, carry):
            newton(ref, False)
            return carry

        lax.fori_loop(1, ITERS - 1, newton_step, 0)
        newton(ref, True)

    rows_out = inv_ref.shape[1]
    half_rows = BLK // 2
    out_start = pl.multiple_of(dp * rows_out, rows_out)

    @pl.when(jnp.logical_not(is_grad))
    def _():
        first_iterate(few, 0, rows_out, out_start)
        first_iterate(few, rows_out, half_rows, pl.multiple_of(xh * half_rows, half_rows))
        iterations(few)
        inv_low[pl.ds(0, half_rows), :] = (few[pl.ds(rows_out, half_rows), :] * scale).astype(BF16)
        inv_ref[0] = few[pl.ds(0, rows_out), :] * scale

    @pl.when(is_grad)
    def _():
        first_iterate(iterate, 0, BLK, 0)
        iterations(iterate)
        inverse = iterate[...] * scale
        iterate[...] = inverse
        inv_low[...] = inverse.astype(BF16)
        inv_ref[0] = iterate[pl.ds(out_start, rows_out), :]

    pieces = inv_act.shape[0]
    piece = inv_act.shape[1]

    def inv_copy(route, rooted, index):
        start = pl.multiple_of(index * piece, piece)
        return pltpu.make_async_remote_copy(
            src_ref=inv_low.at[pl.ds(start, piece)] if rooted else inv_act.at[index],
            dst_ref=inv_act.at[index],
            send_sem=inv_send.at[route, index],
            recv_sem=inv_recv.at[index],
            device_id=routes[route][1],
            device_id_type=MESH,
        )

    def inv_forward(rooted, index):
        for route, (taken, _) in enumerate(routes):
            @pl.when(taken)
            def _():
                inv_copy(route, rooted, index).start()

    def inv_step(index, carry):
        @pl.when(is_root)
        def _():
            inv_forward(True, index)

        @pl.when(receives)
        def _():
            inv_copy(3, False, index).wait_recv()
            inv_forward(False, index)

        return carry

    lax.fori_loop(0, pieces, inv_step, 0)

    def out_place(unit):
        column = 4 * grad + unit
        return column // 3, column % 3

    def out_copy(unit):
        target, slot = out_place(unit)
        return pltpu.make_async_remote_copy(
            src_ref=part.at[unit],
            dst_ref=landed.at[slot],
            send_sem=out_send.at[unit],
            recv_sem=out_recv.at[slot],
            device_id=(dp, target),
            device_id_type=MESH,
        )

    def out_local(unit):
        _, slot = out_place(unit)
        return pltpu.make_async_copy(part.at[unit], landed.at[slot], out_recv.at[slot])

    @pl.when(is_grad)
    def _():
        cross_copy.wait_recv()
        whole = (cross[...] + cross_in[...].astype(F32)).astype(BF16)
        right[...] = dot(whole, inv_low[...]).astype(BF16)
        left = inv_act[...].reshape(pieces * piece, BLK)
        for unit in range(4):
            block = dot(left, right[:, unit * UNIT:(unit + 1) * UNIT])
            part[unit] = block.astype(BF16)
            target, _ = out_place(unit)

            @pl.when(target != owner)
            def _():
                out_copy(unit).start()

            @pl.when(target == owner)
            def _():
                out_local(unit).start()

    for slot in range(3):
        pltpu.make_async_copy(part.at[0], landed.at[slot], out_recv.at[slot]).wait()
        out_ref[:, slot * UNIT:(slot + 1) * UNIT] = landed[slot].astype(F32) * (1.0 / tokens)

    def gather_left(step, carry):
        for way in range(2):
            gather_copy(way, step, 0).wait_send()
        return carry

    lax.fori_loop(0, gather_steps, gather_left, 0)
    for row in range(blocks):
        swap_copy(row).wait_send()

    def chain_left(slot, carry):
        for route, (taken, _) in enumerate(routes):
            @pl.when(taken)
            def _():
                chain_copy(route, act, slot).wait_send()
        return carry

    lax.fori_loop(0, 2 * ny, chain_left, 0)

    def inv_left(index, carry):
        for route, (taken, _) in enumerate(routes):
            @pl.when(taken)
            def _():
                inv_copy(route, False, index).wait_send()
        return carry

    lax.fori_loop(0, pieces, inv_left, 0)

    @pl.when(is_grad)
    def _():
        cross_copy.wait_send()
        for unit in range(4):
            target, _ = out_place(unit)

            @pl.when(target != owner)
            def _():
                out_copy(unit).wait_send()


def per_device(features):
    dp_size = lax.axis_size("dp")
    owner_size = lax.axis_size("owner")
    ny, nz = dp_size // 2, owner_size // 4
    rows = features.shape[0]
    quarter = rows // 4
    pieces = 4
    blocks = BLK // UNIT
    square = (BLK, BLK)
    dma = pltpu.SemaphoreType.DMA
    return pl.pallas_call(
        functools.partial(kernel, ny, nz, rows * dp_size),
        out_shape=(
            jax.ShapeDtypeStruct((1, BLK // dp_size, BLK), F32),
            jax.ShapeDtypeStruct((BLK // 2, 3 * UNIT), F32),
        ),
        in_specs=[pl.BlockSpec(memory_space=pltpu.VMEM)],
        out_specs=[pl.BlockSpec(memory_space=pltpu.VMEM)] * 2,
        scratch_shapes=[
            pltpu.VMEM((4 * ny, quarter, BLK), BF16),
            pltpu.VMEM((4 * ny, quarter, BLK), BF16),
            pltpu.VMEM(square, F32),
            pltpu.VMEM(square, BF16),
            pltpu.VMEM(square, BF16),
            pltpu.VMEM(square, F32),
            pltpu.VMEM(square, BF16),
            pltpu.VMEM(square, BF16),
            pltpu.VMEM(square, F32),
            pltpu.VMEM(square, F32),
            pltpu.VMEM((BLK // dp_size + BLK // 2, BLK), F32),
            pltpu.VMEM(square, BF16),
            pltpu.VMEM((pieces, BLK // 2 // pieces, BLK), BF16),
            pltpu.VMEM(square, BF16),
            pltpu.VMEM((4, BLK // 2, UNIT), BF16),
            pltpu.VMEM((3, BLK // 2, UNIT), BF16),
            dma((2, 2 * (ny - 1))),
            dma((2, 2 * (ny - 1))),
            dma((4, 2 * ny)),
            dma((2 * ny,)),
            dma((blocks + 1,)),
            dma((blocks + 1,)),
            dma((4, pieces)),
            dma((pieces,)),
            dma((4,)),
            dma((3,)),
        ],
        compiler_params=pltpu.CompilerParams(
            collective_id=0, has_side_effects=True, vmem_limit_bytes=48 * 2**20
        ),
    )(features)


def solution(mesh):
    return jax.shard_map(
        per_device,
        mesh=mesh,
        in_specs=(P("dp", "owner"),),
        out_specs=(P("owner", "dp", None), P("dp", "owner")),
        check_vma=False,
    )
```

```python
import functools

import jax
import jax.numpy as jnp
from jax import lax
from jax.experimental import pallas as pl
from jax.experimental.pallas import tpu as pltpu
from jax.sharding import PartitionSpec as P

BLK = 512
ITERS = 6
DAMPING = 0.001
UNIT = 128
MESH = pl.DeviceIdType.MESH
F32 = jnp.float32
BF16 = jnp.bfloat16


def dot(a, b):
    return jnp.dot(a, b, preferred_element_type=F32)


def dot_tn(a, b):
    return lax.dot_general(a, b, (((0,), (0,)), ((), ())), preferred_element_type=F32)


def kernel(
    ny, nz, tokens,
    x_ref, inv_ref, out_ref,
    feat, act, cov, cov_low, cov_in, cross, cross_low, cross_in,
    err, iterate, few, inv_low, inv_act, part, landed,
    gather_send, gather_recv, chain_send, chain_recv, swap_send, swap_recv,
    inv_send, inv_recv, out_send, out_recv,
):
    dp = lax.axis_index("dp")
    owner = lax.axis_index("owner")
    y, xh = dp // 2, dp % 2
    xl, z, core = owner // (2 * nz), (owner // 2) % nz, owner % 2
    rows = x_ref.shape[0]
    quarter = rows // 4
    acts = ny
    gather_steps = (ny - 1) * 2

    def device(y_=y, xh_=xh, xl_=xl, z_=z, core_=core):
        return (y_ * 2 + xh_, xl_ * (2 * nz) + z_ * 2 + core_)

    up, down = device(y_=(y + 1) % ny), device(y_=(y + ny - 1) % ny)
    partner = device(xh_=1 - xh)
    sibling = device(core_=1 - core)

    is_grad = owner >= acts
    grad = owner - acts

    z_next, z_prev = device(z_=(z + 1) % nz), device(z_=(z + nz - 1) % nz)
    flip = device(xl_=1 - xl)
    on_core = core == y % 2
    away = (z + nz - y // 2) % nz
    forth = nz // 2
    is_root = on_core & (away == 0) & (xl == 0)
    has_parent = on_core & jnp.logical_not(is_root)
    parent = jnp.where(away == 0, flip[1], jnp.where(away <= forth, z_prev[1], z_next[1]))
    receives = has_parent | (jnp.logical_not(on_core) & is_grad)
    routes = [
        (on_core & (away < forth), z_next),
        (on_core & ((away == 0) | (away > forth + 1)), z_prev),
        (is_root, flip),
        (on_core & is_grad, sibling),
    ]
    depth = xl + jnp.where(away <= forth, away, nz - away)
    lag = depth + jnp.where(on_core, 0, 1)
    max_depth = 1 + forth
    max_lag = max_depth + 1

    barrier = pltpu.get_barrier_semaphore()
    for other in (up, down, partner):
        pl.semaphore_signal(barrier, inc=1, device_id=other, device_id_type=MESH)

    @pl.when(is_grad)
    def _():
        pl.semaphore_signal(barrier, inc=1, device_id=sibling, device_id_type=MESH)

    @pl.when(has_parent)
    def _():
        pl.semaphore_signal(
            barrier, inc=1, device_id=(dp, parent), device_id_type=MESH
        )

    first_source = acts + (3 * owner) // 4
    last_source = acts + (3 * owner + 2) // 4

    @pl.when(first_source != owner)
    def _():
        pl.semaphore_signal(barrier, inc=1, device_id=(dp, first_source), device_id_type=MESH)

    @pl.when((last_source != owner) & (last_source != first_source))
    def _():
        pl.semaphore_signal(barrier, inc=1, device_id=(dp, last_source), device_id_type=MESH)

    for index in range(4):
        feat[index] = x_ref[pl.ds(index * quarter, quarter), :]
    targets = ((4 * grad) // 3, (4 * grad + 3) // 3)
    peers = sum(jnp.where(is_grad & (target != owner), 1, 0) for target in targets)
    peers = peers + jnp.where(is_grad, 1, 0)
    for taken, _ in routes[:3]:
        peers = peers + jnp.where(taken, 1, 0)
    pl.semaphore_wait(barrier, 3 + peers)

    def gather_copy(way, step, source):
        return pltpu.make_async_remote_copy(
            src_ref=feat.at[source],
            dst_ref=feat.at[4 + 2 * step + way],
            send_sem=gather_send.at[way, step],
            recv_sem=gather_recv.at[way, step],
            device_id=(up, down)[way],
            device_id_type=MESH,
        )

    for step in range(4):
        for way in range(2):
            gather_copy(way, step, step if way == 0 else 3 - step).start()
    own = x_ref[...]
    cov[...] = dot_tn(own, own)

    def chain_copy(route, buffer, slot):
        return pltpu.make_async_remote_copy(
            src_ref=buffer.at[pl.ds(2 * slot, 2)],
            dst_ref=act.at[pl.ds(2 * slot, 2)],
            send_sem=chain_send.at[route, slot],
            recv_sem=chain_recv.at[slot],
            device_id=routes[route][1],
            device_id_type=MESH,
        )

    def chain_forward(buffer, slot):
        for route, (taken, _) in enumerate(routes):
            @pl.when(taken)
            def _():
                chain_copy(route, buffer, slot).start()

    def chain_step(it):
        step = it - lag

        @pl.when((step >= 0) & (step < ny))
        def _():
            for side in range(2):
                slot = 2 * step + side

                @pl.when(is_root)
                def _():
                    chain_forward(feat, slot)

                @pl.when(receives)
                def _():
                    chain_copy(3, act, slot).wait_recv()
                    chain_forward(act, slot)


    def gather_step(it, carry):
        @pl.when(it >= 1)
        def _():
            for half in range(2):
                step = 2 * (it - 1) + half
                for way in range(2):
                    gather_copy(way, step, 0).wait_recv()

                    @pl.when(step + 4 < gather_steps)
                    def _():
                        gather_copy(way, step + 4, 4 + 2 * step + way).start()

        chain_step(it)

        @pl.when(it >= 1)
        def _():
            this = feat[pl.ds(4 * it, 4)].reshape(rows, BLK)
            cov[...] += dot_tn(this, this)

        return carry

    lax.fori_loop(0, ny, gather_step, 0)

    cov_low[...] = cov[...].astype(BF16)

    def swap_copy(row):
        place = (pl.ds(row * UNIT, UNIT), pl.ds(0, (row + 1) * UNIT))
        return pltpu.make_async_remote_copy(
            src_ref=cov_low.at[place],
            dst_ref=cov_in.at[place],
            send_sem=swap_send.at[row],
            recv_sem=swap_recv.at[row],
            device_id=partner,
            device_id_type=MESH,
        )

    blocks = BLK // UNIT
    for row in range(blocks):
        swap_copy(row).start()

    def late_step(it, carry):
        chain_step(it)
        return carry

    lax.fori_loop(ny, ny + max_lag, late_step, 0)

    cross_copy = pltpu.make_async_remote_copy(
        src_ref=cross_low,
        dst_ref=cross_in,
        send_sem=swap_send.at[blocks],
        recv_sem=swap_recv.at[blocks],
        device_id=partner,
        device_id_type=MESH,
    )

    @pl.when(is_grad)
    def _():
        cross[...] = dot_tn(act[...].reshape(ny * rows, BLK), feat[...].reshape(ny * rows, BLK))
        cross_low[...] = cross[...].astype(BF16)
        cross_copy.start()

    for row in range(blocks):
        swap_copy(row).wait_recv()
        rows = pl.ds(row * UNIT, UNIT)
        for col in range(row + 1):
            cols = pl.ds(col * UNIT, UNIT)
            tile = (cov[rows, cols] + cov_in[rows, cols].astype(F32)) * (1.0 / tokens)
            if col == row:
                i = lax.broadcasted_iota(jnp.int32, (UNIT, UNIT), 0)
                j = lax.broadcasted_iota(jnp.int32, (UNIT, UNIT), 1)
                tile = tile + jnp.where(i == j, DAMPING, 0.0)
            err[rows, cols] = tile
            if col < row:
                err[cols, rows] = tile.T
    bound = jnp.max(jnp.sum(jnp.abs(err[...]), axis=1, keepdims=True), axis=0, keepdims=True)
    scale = 1.0 / bound
    first = err[...] * scale
    err[...] = first

    def first_iterate(ref, offset, count, start):
        i = lax.broadcasted_iota(jnp.int32, (count, BLK), 0) + start
        j = lax.broadcasted_iota(jnp.int32, (count, BLK), 1)
        ref[pl.ds(offset, count), :] = jnp.where(i == j, 2.0, 0.0) - err[pl.ds(start, count), :]

    def newton(ref, last):
        e = err[...]
        low = e.astype(BF16)
        x = ref[...]
        high = x.astype(BF16)
        rest = (x - high.astype(F32)).astype(BF16)
        ref[...] = 2.0 * x - (dot(high, low) + dot(rest, low))
        if not last:
            err[...] = 2.0 * e - dot(low, low)

    def iterations(ref):
        e = err[...]
        low = e.astype(BF16)
        err[...] = 2.0 * e - dot(low, low)

        def newton_step(k, carry):
            newton(ref, False)
            return carry

        lax.fori_loop(1, ITERS - 1, newton_step, 0)
        newton(ref, True)

    rows_out = inv_ref.shape[1]
    half_rows = BLK // 2
    out_start = pl.multiple_of(dp * rows_out, rows_out)

    @pl.when(jnp.logical_not(is_grad))
    def _():
        first_iterate(few, 0, rows_out, out_start)
        first_iterate(few, rows_out, half_rows, pl.multiple_of(xh * half_rows, half_rows))
        iterations(few)
        inv_low[pl.ds(0, half_rows), :] = (few[pl.ds(rows_out, half_rows), :] * scale).astype(BF16)
        inv_ref[0] = few[pl.ds(0, rows_out), :] * scale

    @pl.when(is_grad)
    def _():
        first_iterate(iterate, 0, BLK, 0)
        iterations(iterate)
        inverse = iterate[...] * scale
        iterate[...] = inverse
        inv_low[...] = inverse.astype(BF16)
        inv_ref[0] = iterate[pl.ds(out_start, rows_out), :]

    pieces = inv_act.shape[0]
    piece = inv_act.shape[1]

    def inv_copy(route, rooted, index):
        start = pl.multiple_of(index * piece, piece)
        return pltpu.make_async_remote_copy(
            src_ref=inv_low.at[pl.ds(start, piece)] if rooted else inv_act.at[index],
            dst_ref=inv_act.at[index],
            send_sem=inv_send.at[route, index],
            recv_sem=inv_recv.at[index],
            device_id=routes[route][1],
            device_id_type=MESH,
        )

    def inv_forward(rooted, index):
        for route, (taken, _) in enumerate(routes):
            @pl.when(taken)
            def _():
                inv_copy(route, rooted, index).start()

    def inv_step(index, carry):
        @pl.when(is_root)
        def _():
            inv_forward(True, index)

        @pl.when(receives)
        def _():
            inv_copy(3, False, index).wait_recv()
            inv_forward(False, index)

        return carry

    lax.fori_loop(0, pieces, inv_step, 0)

    def out_place(unit):
        column = 4 * grad + unit
        return column // 3, column % 3

    def out_copy(unit):
        target, slot = out_place(unit)
        return pltpu.make_async_remote_copy(
            src_ref=part.at[unit],
            dst_ref=landed.at[slot],
            send_sem=out_send.at[unit],
            recv_sem=out_recv.at[slot],
            device_id=(dp, target),
            device_id_type=MESH,
        )

    def out_local(unit):
        _, slot = out_place(unit)
        return pltpu.make_async_copy(part.at[unit], landed.at[slot], out_recv.at[slot])

    @pl.when(is_grad)
    def _():
        cross_copy.wait_recv()
        whole = (cross[...] + cross_in[...].astype(F32)).astype(BF16)
        left = inv_act[...].reshape(pieces * piece, BLK)
        for unit in range(4):
            if unit % 2 == 0:
                pair = slice(unit * UNIT, (unit + 2) * UNIT)
                right = dot(whole, inv_low[:, pair]).astype(BF16)
                both = dot(left, right)
            block = both[:, unit % 2 * UNIT:(unit % 2 + 1) * UNIT]
            part[unit] = block.astype(BF16)
            target, _ = out_place(unit)

            @pl.when(target != owner)
            def _():
                out_copy(unit).start()

            @pl.when(target == owner)
            def _():
                out_local(unit).start()

    def gather_left(step, carry):
        for way in range(2):
            gather_copy(way, step, 0).wait_send()
        return carry

    lax.fori_loop(0, gather_steps, gather_left, 0)
    for row in range(blocks):
        swap_copy(row).wait_send()

    def chain_left(slot, carry):
        for route, (taken, _) in enumerate(routes):
            @pl.when(taken)
            def _():
                chain_copy(route, act, slot).wait_send()
        return carry

    lax.fori_loop(0, 2 * ny, chain_left, 0)

    def inv_left(index, carry):
        for route, (taken, _) in enumerate(routes):
            @pl.when(taken)
            def _():
                inv_copy(route, False, index).wait_send()
        return carry

    lax.fori_loop(0, pieces, inv_left, 0)

    @pl.when(is_grad)
    def _():
        cross_copy.wait_send()

    for slot in range(3):
        pltpu.make_async_copy(part.at[0], landed.at[slot], out_recv.at[slot]).wait()
        out_ref[:, slot * UNIT:(slot + 1) * UNIT] = landed[slot].astype(F32) * (1.0 / tokens)

    @pl.when(is_grad)
    def _():
        for unit in range(4):
            target, _ = out_place(unit)

            @pl.when(target != owner)
            def _():
                out_copy(unit).wait_send()


def per_device(features):
    dp_size = lax.axis_size("dp")
    owner_size = lax.axis_size("owner")
    ny, nz = dp_size // 2, owner_size // 4
    rows = features.shape[0]
    quarter = rows // 4
    pieces = 4
    blocks = BLK // UNIT
    square = (BLK, BLK)
    dma = pltpu.SemaphoreType.DMA
    return pl.pallas_call(
        functools.partial(kernel, ny, nz, rows * dp_size),
        out_shape=(
            jax.ShapeDtypeStruct((1, BLK // dp_size, BLK), F32),
            jax.ShapeDtypeStruct((BLK // 2, 3 * UNIT), F32),
        ),
        in_specs=[pl.BlockSpec(memory_space=pltpu.VMEM)],
        out_specs=[pl.BlockSpec(memory_space=pltpu.VMEM)] * 2,
        scratch_shapes=[
            pltpu.VMEM((4 * ny, quarter, BLK), BF16),
            pltpu.VMEM((4 * ny, quarter, BLK), BF16),
            pltpu.VMEM(square, F32),
            pltpu.VMEM(square, BF16),
            pltpu.VMEM(square, BF16),
            pltpu.VMEM(square, F32),
            pltpu.VMEM(square, BF16),
            pltpu.VMEM(square, BF16),
            pltpu.VMEM(square, F32),
            pltpu.VMEM(square, F32),
            pltpu.VMEM((BLK // dp_size + BLK // 2, BLK), F32),
            pltpu.VMEM(square, BF16),
            pltpu.VMEM((pieces, BLK // 2 // pieces, BLK), BF16),
            pltpu.VMEM((4, BLK // 2, UNIT), BF16),
            pltpu.VMEM((3, BLK // 2, UNIT), BF16),
            dma((2, 2 * (ny - 1))),
            dma((2, 2 * (ny - 1))),
            dma((4, 2 * ny)),
            dma((2 * ny,)),
            dma((blocks + 1,)),
            dma((blocks + 1,)),
            dma((4, pieces)),
            dma((pieces,)),
            dma((4,)),
            dma((3,)),
        ],
        compiler_params=pltpu.CompilerParams(
            collective_id=0, has_side_effects=True, vmem_limit_bytes=48 * 2**20
        ),
    )(features)


def solution(mesh):
    return jax.shard_map(
        per_device,
        mesh=mesh,
        in_specs=(P("dp", "owner"),),
        out_specs=(P("owner", "dp", None), P("dp", "owner")),
        check_vma=False,
    )
```

```python
import functools

import jax
import jax.numpy as jnp
from jax import lax
from jax.experimental import pallas as pl
from jax.experimental.pallas import tpu as pltpu
from jax.sharding import PartitionSpec as P

BLK = 512
ITERS = 6
DAMPING = 0.001
UNIT = 128
MESH = pl.DeviceIdType.MESH
F32 = jnp.float32
BF16 = jnp.bfloat16


def dot(a, b):
    return jnp.dot(a, b, preferred_element_type=F32)


def dot_tn(a, b):
    return lax.dot_general(a, b, (((0,), (0,)), ((), ())), preferred_element_type=F32)


def kernel(
    ny, nz, tokens,
    x_ref, inv_ref, out_ref,
    feat, act, cov, cov_low, cov_in, cross, cross_low, cross_in,
    err, iterate, few, inv_low, inv_act, right, part, landed,
    gather_send, gather_recv, chain_send, chain_recv, swap_send, swap_recv,
    inv_send, inv_recv, out_send, out_recv,
):
    dp = lax.axis_index("dp")
    owner = lax.axis_index("owner")
    y, xh = dp // 2, dp % 2
    xl, z, core = owner // (2 * nz), (owner // 2) % nz, owner % 2
    rows = x_ref.shape[0]
    quarter = rows // 4
    acts = ny
    gather_steps = (ny - 1) * 2

    def device(y_=y, xh_=xh, xl_=xl, z_=z, core_=core):
        return (y_ * 2 + xh_, xl_ * (2 * nz) + z_ * 2 + core_)

    up, down = device(y_=(y + 1) % ny), device(y_=(y + ny - 1) % ny)
    partner = device(xh_=1 - xh)
    sibling = device(core_=1 - core)

    is_grad = owner >= acts
    grad = owner - acts

    z_next, z_prev = device(z_=(z + 1) % nz), device(z_=(z + nz - 1) % nz)
    flip = device(xl_=1 - xl)
    on_core = core == y % 2
    away = (z + nz - y // 2) % nz
    forth = nz // 2
    is_root = on_core & (away == 0) & (xl == 0)
    has_parent = on_core & jnp.logical_not(is_root)
    parent = jnp.where(away == 0, flip[1], jnp.where(away <= forth, z_prev[1], z_next[1]))
    receives = has_parent | (jnp.logical_not(on_core) & is_grad)
    routes = [
        (on_core & (away < forth), z_next),
        (on_core & ((away == 0) | (away > forth + 1)), z_prev),
        (is_root, flip),
        (on_core & is_grad, sibling),
    ]
    depth = xl + jnp.where(away <= forth, away, nz - away)
    lag = depth + jnp.where(on_core, 0, 1)
    max_depth = 1 + forth
    max_lag = max_depth + 1

    barrier = pltpu.get_barrier_semaphore()
    for other in (up, down, partner):
        pl.semaphore_signal(barrier, inc=1, device_id=other, device_id_type=MESH)

    @pl.when(is_grad)
    def _():
        pl.semaphore_signal(barrier, inc=1, device_id=sibling, device_id_type=MESH)

    @pl.when(has_parent)
    def _():
        pl.semaphore_signal(
            barrier, inc=1, device_id=(dp, parent), device_id_type=MESH
        )

    first_source = acts + (3 * owner) // 4
    last_source = acts + (3 * owner + 2) // 4

    @pl.when(first_source != owner)
    def _():
        pl.semaphore_signal(barrier, inc=1, device_id=(dp, first_source), device_id_type=MESH)

    @pl.when((last_source != owner) & (last_source != first_source))
    def _():
        pl.semaphore_signal(barrier, inc=1, device_id=(dp, last_source), device_id_type=MESH)

    for index in range(4):
        feat[index] = x_ref[pl.ds(index * quarter, quarter), :]
    targets = ((4 * grad) // 3, (4 * grad + 3) // 3)
    peers = sum(jnp.where(is_grad & (target != owner), 1, 0) for target in targets)
    peers = peers + jnp.where(is_grad, 1, 0)
    for taken, _ in routes[:3]:
        peers = peers + jnp.where(taken, 1, 0)
    pl.semaphore_wait(barrier, 3 + peers)

    def gather_copy(way, step, source):
        return pltpu.make_async_remote_copy(
            src_ref=feat.at[source],
            dst_ref=feat.at[4 + 2 * step + way],
            send_sem=gather_send.at[way, step],
            recv_sem=gather_recv.at[way, step],
            device_id=(up, down)[way],
            device_id_type=MESH,
        )

    for step in range(4):
        for way in range(2):
            gather_copy(way, step, step if way == 0 else 3 - step).start()
    own = x_ref[...]
    cov[...] = dot_tn(own, own)

    def chain_copy(route, buffer, slot):
        return pltpu.make_async_remote_copy(
            src_ref=buffer.at[pl.ds(2 * slot, 2)],
            dst_ref=act.at[pl.ds(2 * slot, 2)],
            send_sem=chain_send.at[route, slot],
            recv_sem=chain_recv.at[slot],
            device_id=routes[route][1],
            device_id_type=MESH,
        )

    def chain_forward(buffer, slot):
        for route, (taken, _) in enumerate(routes):
            @pl.when(taken)
            def _():
                chain_copy(route, buffer, slot).start()

    def chain_step(it):
        step = it - lag

        @pl.when((step >= 0) & (step < ny))
        def _():
            for side in range(2):
                slot = 2 * step + side

                @pl.when(is_root)
                def _():
                    chain_forward(feat, slot)

                @pl.when(receives)
                def _():
                    chain_copy(3, act, slot).wait_recv()
                    chain_forward(act, slot)


    def gather_step(it, carry):
        @pl.when(it >= 1)
        def _():
            for half in range(2):
                step = 2 * (it - 1) + half
                for way in range(2):
                    gather_copy(way, step, 0).wait_recv()

                    @pl.when(step + 4 < gather_steps)
                    def _():
                        gather_copy(way, step + 4, 4 + 2 * step + way).start()

        chain_step(it)

        @pl.when(it >= 1)
        def _():
            this = feat[pl.ds(4 * it, 4)].reshape(rows, BLK)
            cov[...] += dot_tn(this, this)

        return carry

    lax.fori_loop(0, ny, gather_step, 0)

    cov_low[...] = cov[...].astype(BF16)

    def swap_copy(row):
        place = (pl.ds(row * UNIT, UNIT), pl.ds(0, (row + 1) * UNIT))
        return pltpu.make_async_remote_copy(
            src_ref=cov_low.at[place],
            dst_ref=cov_in.at[place],
            send_sem=swap_send.at[row],
            recv_sem=swap_recv.at[row],
            device_id=partner,
            device_id_type=MESH,
        )

    blocks = BLK // UNIT
    for row in range(blocks):
        swap_copy(row).start()

    def late_step(it, carry):
        chain_step(it)
        return carry

    lax.fori_loop(ny, ny + max_lag, late_step, 0)

    def cross_copy(row):
        place = pl.ds(row * UNIT, UNIT)
        return pltpu.make_async_remote_copy(
            src_ref=cross_low.at[place],
            dst_ref=cross_in.at[place],
            send_sem=swap_send.at[blocks + row],
            recv_sem=swap_recv.at[blocks + row],
            device_id=partner,
            device_id_type=MESH,
        )

    @pl.when(is_grad)
    def _():
        this = feat[...].reshape(ny * rows, BLK)
        for row in range(blocks):
            place = pl.ds(row * UNIT, UNIT)
            block = dot_tn(act[:, :, place].reshape(ny * rows, UNIT), this)
            cross[place, :] = block
            cross_low[place, :] = block.astype(BF16)
            cross_copy(row).start()

    for row in range(blocks):
        swap_copy(row).wait_recv()
        rows = pl.ds(row * UNIT, UNIT)
        for col in range(row + 1):
            cols = pl.ds(col * UNIT, UNIT)
            tile = (cov[rows, cols] + cov_in[rows, cols].astype(F32)) * (1.0 / tokens)
            if col == row:
                i = lax.broadcasted_iota(jnp.int32, (UNIT, UNIT), 0)
                j = lax.broadcasted_iota(jnp.int32, (UNIT, UNIT), 1)
                tile = tile + jnp.where(i == j, DAMPING, 0.0)
            err[rows, cols] = tile
            if col < row:
                err[cols, rows] = tile.T
    bound = jnp.max(jnp.sum(jnp.abs(err[...]), axis=1, keepdims=True), axis=0, keepdims=True)
    scale = 1.0 / bound
    first = err[...] * scale
    err[...] = first

    def first_iterate(ref, offset, count, start):
        i = lax.broadcasted_iota(jnp.int32, (count, BLK), 0) + start
        j = lax.broadcasted_iota(jnp.int32, (count, BLK), 1)
        ref[pl.ds(offset, count), :] = jnp.where(i == j, 2.0, 0.0) - err[pl.ds(start, count), :]

    def newton(ref, last):
        e = err[...]
        low = e.astype(BF16)
        x = ref[...]
        high = x.astype(BF16)
        rest = (x - high.astype(F32)).astype(BF16)
        ref[...] = 2.0 * x - (dot(high, low) + dot(rest, low))
        if not last:
            err[...] = 2.0 * e - dot(low, low)

    def iterations(ref):
        e = err[...]
        low = e.astype(BF16)
        err[...] = 2.0 * e - dot(low, low)

        def newton_step(k, carry):
            newton(ref, False)
            return carry

        lax.fori_loop(1, ITERS - 1, newton_step, 0)
        newton(ref, True)

    rows_out = inv_ref.shape[1]
    half_rows = BLK // 2
    out_start = pl.multiple_of(dp * rows_out, rows_out)

    @pl.when(jnp.logical_not(is_grad))
    def _():
        first_iterate(few, 0, rows_out, out_start)
        first_iterate(few, rows_out, half_rows, pl.multiple_of(xh * half_rows, half_rows))
        iterations(few)
        inv_low[pl.ds(0, half_rows), :] = (few[pl.ds(rows_out, half_rows), :] * scale).astype(BF16)
        inv_ref[0] = few[pl.ds(0, rows_out), :] * scale

    pieces = inv_act.shape[0]
    piece = inv_act.shape[1]

    def inv_copy(route, rooted, index):
        start = pl.multiple_of(index * piece, piece)
        return pltpu.make_async_remote_copy(
            src_ref=inv_low.at[pl.ds(start, piece)] if rooted else inv_act.at[index],
            dst_ref=inv_act.at[index],
            send_sem=inv_send.at[route, index],
            recv_sem=inv_recv.at[index],
            device_id=routes[route][1],
            device_id_type=MESH,
        )

    def inv_forward(rooted, index):
        for route, (taken, _) in enumerate(routes):
            @pl.when(taken)
            def _():
                inv_copy(route, rooted, index).start()

    def inv_step(index, carry):
        @pl.when(is_root)
        def _():
            inv_forward(True, index)

        @pl.when(receives)
        def _():
            inv_copy(3, False, index).wait_recv()
            inv_forward(False, index)

        return carry

    near_root = on_core & is_grad & (depth <= 2) & (xl == 1)

    @pl.when(near_root)
    def _():
        lax.fori_loop(0, pieces, inv_step, 0)

    @pl.when(is_grad)
    def _():
        first_iterate(iterate, 0, BLK, 0)
        iterations(iterate)
        inverse = iterate[...] * scale
        iterate[...] = inverse
        inv_low[...] = inverse.astype(BF16)
        inv_ref[0] = iterate[pl.ds(out_start, rows_out), :]

    @pl.when(jnp.logical_not(near_root))
    def _():
        lax.fori_loop(0, pieces, inv_step, 0)

    def out_place(unit):
        column = 4 * grad + unit
        return column // 3, column % 3

    def out_copy(unit):
        target, slot = out_place(unit)
        return pltpu.make_async_remote_copy(
            src_ref=part.at[unit],
            dst_ref=landed.at[slot],
            send_sem=out_send.at[unit],
            recv_sem=out_recv.at[slot],
            device_id=(dp, target),
            device_id_type=MESH,
        )

    def out_local(unit):
        _, slot = out_place(unit)
        return pltpu.make_async_copy(part.at[unit], landed.at[slot], out_recv.at[slot])

    @pl.when(is_grad)
    def _():
        for row in range(blocks):
            cross_copy(row).wait_recv()
            place = pl.ds(row * UNIT, UNIT)
            whole = (cross[place, :] + cross_in[place, :].astype(F32)).astype(BF16)
            right[place, :] = dot(whole, inv_low[...]).astype(BF16)
        left = inv_act[...].reshape(pieces * piece, BLK)
        for unit in (2, 3, 0, 1):
            if unit % 2 == 0:
                pair = slice(unit * UNIT, (unit + 2) * UNIT)
                both = dot(left, right[:, pair])
            block = both[:, unit % 2 * UNIT:(unit % 2 + 1) * UNIT]
            part[unit] = block.astype(BF16)
            target, _ = out_place(unit)

            @pl.when(target != owner)
            def _():
                out_copy(unit).start()

            @pl.when(target == owner)
            def _():
                out_local(unit).start()

    def gather_left(step, carry):
        for way in range(2):
            gather_copy(way, step, 0).wait_send()
        return carry

    lax.fori_loop(0, gather_steps, gather_left, 0)
    for row in range(blocks):
        swap_copy(row).wait_send()

    def chain_left(slot, carry):
        for route, (taken, _) in enumerate(routes):
            @pl.when(taken)
            def _():
                chain_copy(route, act, slot).wait_send()
        return carry

    lax.fori_loop(0, 2 * ny, chain_left, 0)

    def inv_left(index, carry):
        for route, (taken, _) in enumerate(routes):
            @pl.when(taken)
            def _():
                inv_copy(route, False, index).wait_send()
        return carry

    lax.fori_loop(0, pieces, inv_left, 0)

    @pl.when(is_grad)
    def _():
        for row in range(blocks):
            cross_copy(row).wait_send()

    for slot in range(3):
        pltpu.make_async_copy(part.at[0], landed.at[slot], out_recv.at[slot]).wait()
        out_ref[:, slot * UNIT:(slot + 1) * UNIT] = landed[slot].astype(F32) * (1.0 / tokens)

    @pl.when(is_grad)
    def _():
        for unit in range(4):
            target, _ = out_place(unit)

            @pl.when(target != owner)
            def _():
                out_copy(unit).wait_send()


def per_device(features):
    dp_size = lax.axis_size("dp")
    owner_size = lax.axis_size("owner")
    ny, nz = dp_size // 2, owner_size // 4
    rows = features.shape[0]
    quarter = rows // 4
    pieces = 8
    blocks = BLK // UNIT
    square = (BLK, BLK)
    dma = pltpu.SemaphoreType.DMA
    return pl.pallas_call(
        functools.partial(kernel, ny, nz, rows * dp_size),
        out_shape=(
            jax.ShapeDtypeStruct((1, BLK // dp_size, BLK), F32),
            jax.ShapeDtypeStruct((BLK // 2, 3 * UNIT), F32),
        ),
        in_specs=[pl.BlockSpec(memory_space=pltpu.VMEM)],
        out_specs=[pl.BlockSpec(memory_space=pltpu.VMEM)] * 2,
        scratch_shapes=[
            pltpu.VMEM((4 * ny, quarter, BLK), BF16),
            pltpu.VMEM((4 * ny, quarter, BLK), BF16),
            pltpu.VMEM(square, F32),
            pltpu.VMEM(square, BF16),
            pltpu.VMEM(square, BF16),
            pltpu.VMEM(square, F32),
            pltpu.VMEM(square, BF16),
            pltpu.VMEM(square, BF16),
            pltpu.VMEM(square, F32),
            pltpu.VMEM(square, F32),
            pltpu.VMEM((BLK // dp_size + BLK // 2, BLK), F32),
            pltpu.VMEM(square, BF16),
            pltpu.VMEM((pieces, BLK // 2 // pieces, BLK), BF16),
            pltpu.VMEM(square, BF16),
            pltpu.VMEM((4, BLK // 2, UNIT), BF16),
            pltpu.VMEM((3, BLK // 2, UNIT), BF16),
            dma((2, 2 * (ny - 1))),
            dma((2, 2 * (ny - 1))),
            dma((4, 2 * ny)),
            dma((2 * ny,)),
            dma((2 * blocks,)),
            dma((2 * blocks,)),
            dma((4, pieces)),
            dma((pieces,)),
            dma((4,)),
            dma((3,)),
        ],
        compiler_params=pltpu.CompilerParams(
            collective_id=0, has_side_effects=True, vmem_limit_bytes=48 * 2**20
        ),
    )(features)


def solution(mesh):
    return jax.shard_map(
        per_device,
        mesh=mesh,
        in_specs=(P("dp", "owner"),),
        out_specs=(P("owner", "dp", None), P("dp", "owner")),
        check_vma=False,
    )
```

```python
import functools

import jax
import jax.numpy as jnp
from jax import lax
from jax.experimental import pallas as pl
from jax.experimental.pallas import tpu as pltpu
from jax.sharding import PartitionSpec as P

BLK = 512
ITERS = 6
DAMPING = 0.001
UNIT = 128
MESH = pl.DeviceIdType.MESH
F32 = jnp.float32
BF16 = jnp.bfloat16


def dot(a, b):
    return jnp.dot(a, b, preferred_element_type=F32)


def dot_tn(a, b):
    return lax.dot_general(a, b, (((0,), (0,)), ((), ())), preferred_element_type=F32)


def kernel(
    ny, nz, tokens,
    x_ref, inv_ref, out_ref,
    feat, act, cov, cov_low, cov_in, cross, cross_low, cross_in,
    err, iterate, few, inv_low, inv_act, right, part, landed,
    gather_send, gather_recv, chain_send, chain_recv, swap_send, swap_recv,
    inv_send, inv_recv, out_send, out_recv,
):
    dp = lax.axis_index("dp")
    owner = lax.axis_index("owner")
    y, xh = dp // 2, dp % 2
    xl, z, core = owner // (2 * nz), (owner // 2) % nz, owner % 2
    rows = x_ref.shape[0]
    quarter = rows // 4
    acts = ny
    gather_steps = (ny - 1) * 2

    def device(y_=y, xh_=xh, xl_=xl, z_=z, core_=core):
        return (y_ * 2 + xh_, xl_ * (2 * nz) + z_ * 2 + core_)

    up, down = device(y_=(y + 1) % ny), device(y_=(y + ny - 1) % ny)
    partner = device(xh_=1 - xh)
    sibling = device(core_=1 - core)

    is_grad = owner >= acts
    grad = owner - acts

    z_next, z_prev = device(z_=(z + 1) % nz), device(z_=(z + nz - 1) % nz)
    flip = device(xl_=1 - xl)
    on_core = core == y % 2
    away = (z + nz - y // 2) % nz
    forth = nz // 2
    is_root = on_core & (away == 0) & (xl == 0)
    has_parent = on_core & jnp.logical_not(is_root)
    parent = jnp.where(away == 0, flip[1], jnp.where(away <= forth, z_prev[1], z_next[1]))
    receives = has_parent | (jnp.logical_not(on_core) & is_grad)
    routes = [
        (on_core & (away < forth), z_next),
        (on_core & ((away == 0) | (away > forth + 1)), z_prev),
        (is_root, flip),
        (on_core & is_grad, sibling),
    ]
    depth = xl + jnp.where(away <= forth, away, nz - away)
    lag = depth + jnp.where(on_core, 0, 1)
    max_depth = 1 + forth
    max_lag = max_depth + 1

    barrier = pltpu.get_barrier_semaphore()
    for other in (up, down, partner):
        pl.semaphore_signal(barrier, inc=1, device_id=other, device_id_type=MESH)

    @pl.when(is_grad)
    def _():
        pl.semaphore_signal(barrier, inc=1, device_id=sibling, device_id_type=MESH)

    @pl.when(has_parent)
    def _():
        pl.semaphore_signal(
            barrier, inc=1, device_id=(dp, parent), device_id_type=MESH
        )

    first_source = acts + (3 * owner) // 4
    last_source = acts + (3 * owner + 2) // 4

    @pl.when(first_source != owner)
    def _():
        pl.semaphore_signal(barrier, inc=1, device_id=(dp, first_source), device_id_type=MESH)

    @pl.when((last_source != owner) & (last_source != first_source))
    def _():
        pl.semaphore_signal(barrier, inc=1, device_id=(dp, last_source), device_id_type=MESH)

    for index in range(4):
        feat[index] = x_ref[pl.ds(index * quarter, quarter), :]
    targets = ((4 * grad) // 3, (4 * grad + 3) // 3)
    peers = sum(jnp.where(is_grad & (target != owner), 1, 0) for target in targets)
    peers = peers + jnp.where(is_grad, 1, 0)
    for taken, _ in routes[:3]:
        peers = peers + jnp.where(taken, 1, 0)
    pl.semaphore_wait(barrier, 3 + peers)

    def gather_copy(way, step, source):
        return pltpu.make_async_remote_copy(
            src_ref=feat.at[source],
            dst_ref=feat.at[4 + 2 * step + way],
            send_sem=gather_send.at[way, step],
            recv_sem=gather_recv.at[way, step],
            device_id=(up, down)[way],
            device_id_type=MESH,
        )

    for step in range(4):
        for way in range(2):
            gather_copy(way, step, step if way == 0 else 3 - step).start()
    own = x_ref[...]
    cov[...] = dot_tn(own, own)

    def chain_copy(route, buffer, slot):
        return pltpu.make_async_remote_copy(
            src_ref=buffer.at[pl.ds(2 * slot, 2)],
            dst_ref=act.at[pl.ds(2 * slot, 2)],
            send_sem=chain_send.at[route, slot],
            recv_sem=chain_recv.at[slot],
            device_id=routes[route][1],
            device_id_type=MESH,
        )

    def chain_forward(buffer, slot):
        for route, (taken, _) in enumerate(routes):
            @pl.when(taken)
            def _():
                chain_copy(route, buffer, slot).start()

    def chain_step(it):
        step = it - lag

        @pl.when((step >= 0) & (step < ny))
        def _():
            for side in range(2):
                slot = 2 * step + side

                @pl.when(is_root & (step == 0))
                def _():
                    chain_forward(feat, slot)

                @pl.when(receives)
                def _():
                    chain_copy(3, act, slot).wait_recv()
                    chain_forward(act, slot)


    def gather_step(it, carry):
        @pl.when(it >= 1)
        def _():
            for half in range(2):
                step = 2 * (it - 1) + half
                for way in range(2):
                    gather_copy(way, step, 0).wait_recv()

                    @pl.when(step + 4 < gather_steps)
                    def _():
                        gather_copy(way, step + 4, 4 + 2 * step + way).start()

                @pl.when(is_root)
                def _():
                    chain_forward(feat, 2 * it + half)

        chain_step(it)

        @pl.when(it >= 1)
        def _():
            this = feat[pl.ds(4 * it, 4)].reshape(rows, BLK)
            cov[...] += dot_tn(this, this)

        return carry

    lax.fori_loop(0, ny, gather_step, 0)

    cov_low[...] = cov[...].astype(BF16)

    def swap_copy(row):
        place = (pl.ds(row * UNIT, UNIT), pl.ds(0, (row + 1) * UNIT))
        return pltpu.make_async_remote_copy(
            src_ref=cov_low.at[place],
            dst_ref=cov_in.at[place],
            send_sem=swap_send.at[row],
            recv_sem=swap_recv.at[row],
            device_id=partner,
            device_id_type=MESH,
        )

    blocks = BLK // UNIT
    for row in range(blocks):
        swap_copy(row).start()

    def late_step(it, carry):
        chain_step(it)
        return carry

    lax.fori_loop(ny, ny + max_lag, late_step, 0)

    def cross_copy(row):
        place = pl.ds(row * UNIT, UNIT)
        return pltpu.make_async_remote_copy(
            src_ref=cross_low.at[place],
            dst_ref=cross_in.at[place],
            send_sem=swap_send.at[blocks + row],
            recv_sem=swap_recv.at[blocks + row],
            device_id=partner,
            device_id_type=MESH,
        )

    @pl.when(is_grad)
    def _():
        this = feat[...].reshape(ny * rows, BLK)
        for row in range(blocks):
            place = pl.ds(row * UNIT, UNIT)
            block = dot_tn(act[:, :, place].reshape(ny * rows, UNIT), this)
            cross[place, :] = block
            cross_low[place, :] = block.astype(BF16)
            cross_copy(row).start()

    for row in range(blocks):
        swap_copy(row).wait_recv()
        rows = pl.ds(row * UNIT, UNIT)
        for col in range(row + 1):
            cols = pl.ds(col * UNIT, UNIT)
            tile = (cov[rows, cols] + cov_in[rows, cols].astype(F32)) * (1.0 / tokens)
            if col == row:
                i = lax.broadcasted_iota(jnp.int32, (UNIT, UNIT), 0)
                j = lax.broadcasted_iota(jnp.int32, (UNIT, UNIT), 1)
                tile = tile + jnp.where(i == j, DAMPING, 0.0)
            err[rows, cols] = tile
            if col < row:
                err[cols, rows] = tile.T
    bound = jnp.max(jnp.sum(jnp.abs(err[...]), axis=1, keepdims=True), axis=0, keepdims=True)
    scale = 1.0 / bound
    first = err[...] * scale
    err[...] = first

    def first_iterate(ref, offset, count, start):
        i = lax.broadcasted_iota(jnp.int32, (count, BLK), 0) + start
        j = lax.broadcasted_iota(jnp.int32, (count, BLK), 1)
        ref[pl.ds(offset, count), :] = jnp.where(i == j, 2.0, 0.0) - err[pl.ds(start, count), :]

    def newton(ref, last):
        e = err[...]
        low = e.astype(BF16)
        x = ref[...]
        high = x.astype(BF16)
        rest = (x - high.astype(F32)).astype(BF16)
        ref[...] = 2.0 * x - (dot(high, low) + dot(rest, low))
        if not last:
            err[...] = 2.0 * e - dot(low, low)

    def iterations(ref):
        e = err[...]
        low = e.astype(BF16)
        err[...] = 2.0 * e - dot(low, low)

        def newton_step(k, carry):
            newton(ref, False)
            return carry

        lax.fori_loop(1, ITERS - 1, newton_step, 0)
        newton(ref, True)

    rows_out = inv_ref.shape[1]
    half_rows = BLK // 2
    out_start = pl.multiple_of(dp * rows_out, rows_out)

    @pl.when(jnp.logical_not(is_grad))
    def _():
        first_iterate(few, 0, rows_out, out_start)
        first_iterate(few, rows_out, half_rows, pl.multiple_of(xh * half_rows, half_rows))
        iterations(few)
        inv_low[pl.ds(0, half_rows), :] = (few[pl.ds(rows_out, half_rows), :] * scale).astype(BF16)
        inv_ref[0] = few[pl.ds(0, rows_out), :] * scale

    pieces = inv_act.shape[0]
    piece = inv_act.shape[1]

    def inv_copy(route, rooted, index):
        start = pl.multiple_of(index * piece, piece)
        return pltpu.make_async_remote_copy(
            src_ref=inv_low.at[pl.ds(start, piece)] if rooted else inv_act.at[index],
            dst_ref=inv_act.at[index],
            send_sem=inv_send.at[route, index],
            recv_sem=inv_recv.at[index],
            device_id=routes[route][1],
            device_id_type=MESH,
        )

    def inv_forward(rooted, index):
        for route, (taken, _) in enumerate(routes):
            @pl.when(taken)
            def _():
                inv_copy(route, rooted, index).start()

    def inv_step(index, carry):
        @pl.when(is_root)
        def _():
            inv_forward(True, index)

        @pl.when(receives)
        def _():
            inv_copy(3, False, index).wait_recv()
            inv_forward(False, index)

        return carry

    near_root = on_core & is_grad & (depth <= 2) & (xl == 1)

    @pl.when(near_root)
    def _():
        lax.fori_loop(0, pieces, inv_step, 0)

    @pl.when(is_grad)
    def _():
        first_iterate(iterate, 0, BLK, 0)
        iterations(iterate)
        inverse = iterate[...] * scale
        iterate[...] = inverse
        inv_low[...] = inverse.astype(BF16)
        inv_ref[0] = iterate[pl.ds(out_start, rows_out), :]

    @pl.when(jnp.logical_not(near_root))
    def _():
        lax.fori_loop(0, pieces, inv_step, 0)

    def out_place(unit):
        column = 4 * grad + unit
        return column // 3, column % 3

    def out_copy(unit):
        target, slot = out_place(unit)
        return pltpu.make_async_remote_copy(
            src_ref=part.at[unit],
            dst_ref=landed.at[slot],
            send_sem=out_send.at[unit],
            recv_sem=out_recv.at[slot],
            device_id=(dp, target),
            device_id_type=MESH,
        )

    def out_local(unit):
        _, slot = out_place(unit)
        return pltpu.make_async_copy(part.at[unit], landed.at[slot], out_recv.at[slot])

    @pl.when(is_grad)
    def _():
        for row in range(blocks):
            cross_copy(row).wait_recv()
            place = pl.ds(row * UNIT, UNIT)
            whole = (cross[place, :] + cross_in[place, :].astype(F32)).astype(BF16)
            right[place, :] = dot(whole, inv_low[...]).astype(BF16)
        left = inv_act[...].reshape(pieces * piece, BLK)
        for unit in (2, 3, 0, 1):
            if unit % 2 == 0:
                pair = slice(unit * UNIT, (unit + 2) * UNIT)
                both = dot(left, right[:, pair])
            block = both[:, unit % 2 * UNIT:(unit % 2 + 1) * UNIT]
            part[unit] = block.astype(BF16)
            target, _ = out_place(unit)

            @pl.when(target != owner)
            def _():
                out_copy(unit).start()

            @pl.when(target == owner)
            def _():
                out_local(unit).start()

    def gather_left(step, carry):
        for way in range(2):
            gather_copy(way, step, 0).wait_send()
        return carry

    lax.fori_loop(0, gather_steps, gather_left, 0)
    for row in range(blocks):
        swap_copy(row).wait_send()

    def chain_left(slot, carry):
        for route, (taken, _) in enumerate(routes):
            @pl.when(taken)
            def _():
                chain_copy(route, act, slot).wait_send()
        return carry

    lax.fori_loop(0, 2 * ny, chain_left, 0)

    def inv_left(index, carry):
        for route, (taken, _) in enumerate(routes):
            @pl.when(taken)
            def _():
                inv_copy(route, False, index).wait_send()
        return carry

    lax.fori_loop(0, pieces, inv_left, 0)

    @pl.when(is_grad)
    def _():
        for row in range(blocks):
            cross_copy(row).wait_send()

    for slot in range(3):
        pltpu.make_async_copy(part.at[0], landed.at[slot], out_recv.at[slot]).wait()
        out_ref[:, slot * UNIT:(slot + 1) * UNIT] = landed[slot].astype(F32) * (1.0 / tokens)

    @pl.when(is_grad)
    def _():
        for unit in range(4):
            target, _ = out_place(unit)

            @pl.when(target != owner)
            def _():
                out_copy(unit).wait_send()


def per_device(features):
    dp_size = lax.axis_size("dp")
    owner_size = lax.axis_size("owner")
    ny, nz = dp_size // 2, owner_size // 4
    rows = features.shape[0]
    quarter = rows // 4
    pieces = 8
    blocks = BLK // UNIT
    square = (BLK, BLK)
    dma = pltpu.SemaphoreType.DMA
    return pl.pallas_call(
        functools.partial(kernel, ny, nz, rows * dp_size),
        out_shape=(
            jax.ShapeDtypeStruct((1, BLK // dp_size, BLK), F32),
            jax.ShapeDtypeStruct((BLK // 2, 3 * UNIT), F32),
        ),
        in_specs=[pl.BlockSpec(memory_space=pltpu.VMEM)],
        out_specs=[pl.BlockSpec(memory_space=pltpu.VMEM)] * 2,
        scratch_shapes=[
            pltpu.VMEM((4 * ny, quarter, BLK), BF16),
            pltpu.VMEM((4 * ny, quarter, BLK), BF16),
            pltpu.VMEM(square, F32),
            pltpu.VMEM(square, BF16),
            pltpu.VMEM(square, BF16),
            pltpu.VMEM(square, F32),
            pltpu.VMEM(square, BF16),
            pltpu.VMEM(square, BF16),
            pltpu.VMEM(square, F32),
            pltpu.VMEM(square, F32),
            pltpu.VMEM((BLK // dp_size + BLK // 2, BLK), F32),
            pltpu.VMEM(square, BF16),
            pltpu.VMEM((pieces, BLK // 2 // pieces, BLK), BF16),
            pltpu.VMEM(square, BF16),
            pltpu.VMEM((4, BLK // 2, UNIT), BF16),
            pltpu.VMEM((3, BLK // 2, UNIT), BF16),
            dma((2, 2 * (ny - 1))),
            dma((2, 2 * (ny - 1))),
            dma((4, 2 * ny)),
            dma((2 * ny,)),
            dma((2 * blocks,)),
            dma((2 * blocks,)),
            dma((4, pieces)),
            dma((pieces,)),
            dma((4,)),
            dma((3,)),
        ],
        compiler_params=pltpu.CompilerParams(
            collective_id=0, has_side_effects=True, vmem_limit_bytes=48 * 2**20
        ),
    )(features)


def solution(mesh):
    return jax.shard_map(
        per_device,
        mesh=mesh,
        in_specs=(P("dp", "owner"),),
        out_specs=(P("owner", "dp", None), P("dp", "owner")),
        check_vma=False,
    )
```

```python
import functools

import jax
import jax.numpy as jnp
from jax import lax
from jax.experimental import pallas as pl
from jax.experimental.pallas import tpu as pltpu
from jax.sharding import PartitionSpec as P

BLK = 512
ITERS = 6
DAMPING = 0.001
UNIT = 128
MESH = pl.DeviceIdType.MESH
F32 = jnp.float32
BF16 = jnp.bfloat16


def dot(a, b):
    return jnp.dot(a, b, preferred_element_type=F32)


def dot_tn(a, b):
    return lax.dot_general(a, b, (((0,), (0,)), ((), ())), preferred_element_type=F32)


def kernel(
    ny, nz, tokens,
    x_ref, inv_ref, out_ref,
    feat, act, cov, cov_low, cov_in, cross, cross_low, cross_in,
    err, iterate, few, inv_low, inv_act, part, landed,
    gather_send, gather_recv, chain_send, chain_recv, swap_send, swap_recv,
    inv_send, inv_recv, out_send, out_recv,
):
    dp = lax.axis_index("dp")
    owner = lax.axis_index("owner")
    y, xh = dp // 2, dp % 2
    xl, z, core = owner // (2 * nz), (owner // 2) % nz, owner % 2
    rows = x_ref.shape[0]
    quarter = rows // 4
    acts = ny
    gather_steps = (ny - 1) * 2

    def device(y_=y, xh_=xh, xl_=xl, z_=z, core_=core):
        return (y_ * 2 + xh_, xl_ * (2 * nz) + z_ * 2 + core_)

    up, down = device(y_=(y + 1) % ny), device(y_=(y + ny - 1) % ny)
    partner = device(xh_=1 - xh)
    sibling = device(core_=1 - core)

    is_grad = owner >= acts
    grad = owner - acts

    z_next, z_prev = device(z_=(z + 1) % nz), device(z_=(z + nz - 1) % nz)
    flip = device(xl_=1 - xl)
    on_core = core == y % 2
    away = (z + nz - y // 2) % nz
    forth = nz // 2
    is_root = on_core & (away == 0) & (xl == 0)
    has_parent = on_core & jnp.logical_not(is_root)
    parent = jnp.where(away == 0, flip[1], jnp.where(away <= forth, z_prev[1], z_next[1]))
    receives = has_parent | (jnp.logical_not(on_core) & is_grad)
    routes = [
        (on_core & (away < forth), z_next),
        (on_core & ((away == 0) | (away > forth + 1)), z_prev),
        (is_root, flip),
        (on_core & is_grad, sibling),
    ]
    depth = xl + jnp.where(away <= forth, away, nz - away)
    lag = depth + jnp.where(on_core, 0, 1)
    max_depth = 1 + forth
    max_lag = max_depth + 1

    barrier = pltpu.get_barrier_semaphore()
    for other in (up, down, partner):
        pl.semaphore_signal(barrier, inc=1, device_id=other, device_id_type=MESH)

    @pl.when(is_grad)
    def _():
        pl.semaphore_signal(barrier, inc=1, device_id=sibling, device_id_type=MESH)

    @pl.when(has_parent)
    def _():
        pl.semaphore_signal(
            barrier, inc=1, device_id=(dp, parent), device_id_type=MESH
        )

    first_source = acts + (3 * owner) // 4
    last_source = acts + (3 * owner + 2) // 4

    @pl.when(first_source != owner)
    def _():
        pl.semaphore_signal(barrier, inc=1, device_id=(dp, first_source), device_id_type=MESH)

    @pl.when((last_source != owner) & (last_source != first_source))
    def _():
        pl.semaphore_signal(barrier, inc=1, device_id=(dp, last_source), device_id_type=MESH)

    for index in range(4):
        feat[index] = x_ref[pl.ds(index * quarter, quarter), :]
    targets = ((4 * grad) // 3, (4 * grad + 3) // 3)
    peers = sum(jnp.where(is_grad & (target != owner), 1, 0) for target in targets)
    peers = peers + jnp.where(is_grad, 1, 0)
    for taken, _ in routes[:3]:
        peers = peers + jnp.where(taken, 1, 0)
    pl.semaphore_wait(barrier, 3 + peers)

    def gather_copy(way, step, source):
        return pltpu.make_async_remote_copy(
            src_ref=feat.at[source],
            dst_ref=feat.at[4 + 2 * step + way],
            send_sem=gather_send.at[way, step],
            recv_sem=gather_recv.at[way, step],
            device_id=(up, down)[way],
            device_id_type=MESH,
        )

    for step in range(4):
        for way in range(2):
            gather_copy(way, step, step if way == 0 else 3 - step).start()
    own = x_ref[...]
    cov[...] = dot_tn(own, own)

    def chain_copy(route, buffer, slot):
        return pltpu.make_async_remote_copy(
            src_ref=buffer.at[pl.ds(2 * slot, 2)],
            dst_ref=act.at[pl.ds(2 * slot, 2)],
            send_sem=chain_send.at[route, slot],
            recv_sem=chain_recv.at[slot],
            device_id=routes[route][1],
            device_id_type=MESH,
        )

    def chain_forward(buffer, slot):
        for route, (taken, _) in enumerate(routes):
            @pl.when(taken)
            def _():
                chain_copy(route, buffer, slot).start()

    def chain_step(it):
        step = it - lag

        @pl.when((step >= 0) & (step < ny))
        def _():
            for side in range(2):
                slot = 2 * step + side

                @pl.when(is_root)
                def _():
                    chain_forward(feat, slot)

                @pl.when(receives)
                def _():
                    chain_copy(3, act, slot).wait_recv()
                    chain_forward(act, slot)


    def gather_step(it, carry):
        @pl.when(it >= 1)
        def _():
            for half in range(2):
                step = 2 * (it - 1) + half
                for way in range(2):
                    gather_copy(way, step, 0).wait_recv()

                    @pl.when(step + 4 < gather_steps)
                    def _():
                        gather_copy(way, step + 4, 4 + 2 * step + way).start()

        chain_step(it)

        @pl.when(it >= 1)
        def _():
            this = feat[pl.ds(4 * it, 4)].reshape(rows, BLK)
            cov[...] += dot_tn(this, this)

        return carry

    lax.fori_loop(0, ny, gather_step, 0)

    cov_low[...] = cov[...].astype(BF16)

    def swap_copy(row):
        place = (pl.ds(row * UNIT, UNIT), pl.ds(0, (row + 1) * UNIT))
        return pltpu.make_async_remote_copy(
            src_ref=cov_low.at[place],
            dst_ref=cov_in.at[place],
            send_sem=swap_send.at[row],
            recv_sem=swap_recv.at[row],
            device_id=partner,
            device_id_type=MESH,
        )

    blocks = BLK // UNIT
    for row in range(blocks):
        swap_copy(row).start()

    def late_step(it, carry):
        chain_step(it)
        return carry

    lax.fori_loop(ny, ny + max_lag, late_step, 0)

    cross_copy = pltpu.make_async_remote_copy(
        src_ref=cross_low,
        dst_ref=cross_in,
        send_sem=swap_send.at[blocks],
        recv_sem=swap_recv.at[blocks],
        device_id=partner,
        device_id_type=MESH,
    )

    @pl.when(is_grad)
    def _():
        cross[...] = dot_tn(act[...].reshape(ny * rows, BLK), feat[...].reshape(ny * rows, BLK))
        cross_low[...] = cross[...].astype(BF16)
        cross_copy.start()

    for row in range(blocks):
        swap_copy(row).wait_recv()
        rows = pl.ds(row * UNIT, UNIT)
        for col in range(row + 1):
            cols = pl.ds(col * UNIT, UNIT)
            tile = (cov[rows, cols] + cov_in[rows, cols].astype(F32)) * (1.0 / tokens)
            if col == row:
                i = lax.broadcasted_iota(jnp.int32, (UNIT, UNIT), 0)
                j = lax.broadcasted_iota(jnp.int32, (UNIT, UNIT), 1)
                tile = tile + jnp.where(i == j, DAMPING, 0.0)
            err[rows, cols] = tile
            if col < row:
                err[cols, rows] = tile.T
    bound = jnp.max(jnp.sum(jnp.abs(err[...]), axis=1, keepdims=True), axis=0, keepdims=True)
    scale = 1.0 / bound
    first = err[...] * scale
    err[...] = first

    def first_iterate(ref, offset, count, start):
        i = lax.broadcasted_iota(jnp.int32, (count, BLK), 0) + start
        j = lax.broadcasted_iota(jnp.int32, (count, BLK), 1)
        ref[pl.ds(offset, count), :] = jnp.where(i == j, 2.0, 0.0) - err[pl.ds(start, count), :]

    def newton(ref, last):
        e = err[...]
        low = e.astype(BF16)
        x = ref[...]
        high = x.astype(BF16)
        rest = (x - high.astype(F32)).astype(BF16)
        ref[...] = 2.0 * x - (dot(high, low) + dot(rest, low))
        if not last:
            err[...] = 2.0 * e - dot(low, low)

    def iterations(ref):
        e = err[...]
        low = e.astype(BF16)
        err[...] = 2.0 * e - dot(low, low)

        def newton_step(k, carry):
            newton(ref, False)
            return carry

        lax.fori_loop(1, ITERS - 1, newton_step, 0)
        newton(ref, True)

    rows_out = inv_ref.shape[1]
    half_rows = BLK // 2
    out_start = pl.multiple_of(dp * rows_out, rows_out)

    @pl.when(jnp.logical_not(is_grad))
    def _():
        first_iterate(few, 0, rows_out, out_start)
        first_iterate(few, rows_out, half_rows, pl.multiple_of(xh * half_rows, half_rows))
        iterations(few)
        inv_low[pl.ds(0, half_rows), :] = (few[pl.ds(rows_out, half_rows), :] * scale).astype(BF16)
        inv_ref[0] = few[pl.ds(0, rows_out), :] * scale

    @pl.when(is_grad)
    def _():
        first_iterate(iterate, 0, BLK, 0)
        iterations(iterate)
        inverse = iterate[...] * scale
        iterate[...] = inverse
        inv_low[...] = inverse.astype(BF16)
        inv_ref[0] = iterate[pl.ds(out_start, rows_out), :]

    pieces = inv_act.shape[0]
    piece = inv_act.shape[1]

    def inv_copy(route, rooted, index):
        start = pl.multiple_of(index * piece, piece)
        return pltpu.make_async_remote_copy(
            src_ref=inv_low.at[pl.ds(start, piece)] if rooted else inv_act.at[index],
            dst_ref=inv_act.at[index],
            send_sem=inv_send.at[route, index],
            recv_sem=inv_recv.at[index],
            device_id=routes[route][1],
            device_id_type=MESH,
        )

    def inv_forward(rooted, index):
        for route, (taken, _) in enumerate(routes):
            @pl.when(taken)
            def _():
                inv_copy(route, rooted, index).start()

    def inv_step(index, carry):
        @pl.when(is_root)
        def _():
            inv_forward(True, index)

        @pl.when(receives)
        def _():
            inv_copy(3, False, index).wait_recv()
            inv_forward(False, index)

        return carry

    lax.fori_loop(0, pieces, inv_step, 0)

    def out_place(unit):
        column = 4 * grad + unit
        return column // 3, column % 3

    def out_copy(unit):
        target, slot = out_place(unit)
        return pltpu.make_async_remote_copy(
            src_ref=part.at[unit],
            dst_ref=landed.at[slot],
            send_sem=out_send.at[unit],
            recv_sem=out_recv.at[slot],
            device_id=(dp, target),
            device_id_type=MESH,
        )

    def out_local(unit):
        _, slot = out_place(unit)
        return pltpu.make_async_copy(part.at[unit], landed.at[slot], out_recv.at[slot])

    @pl.when(is_grad)
    def _():
        cross_copy.wait_recv()
        whole = (cross[...] + cross_in[...].astype(F32)).astype(BF16)
        left = inv_act[...].reshape(pieces * piece, BLK)
        for unit in range(4):
            if unit % 2 == 0:
                pair = slice(unit * UNIT, (unit + 2) * UNIT)
                right = dot(whole, inv_low[:, pair]).astype(BF16)
                both = dot(left, right)
            block = both[:, unit % 2 * UNIT:(unit % 2 + 1) * UNIT]
            part[unit] = block.astype(BF16)
            target, _ = out_place(unit)

            @pl.when(target != owner)
            def _():
                out_copy(unit).start()

            @pl.when(target == owner)
            def _():
                out_local(unit).start()

    def gather_left(step, carry):
        for way in range(2):
            gather_copy(way, step, 0).wait_send()
        return carry

    lax.fori_loop(0, gather_steps, gather_left, 0)
    for row in range(blocks):
        swap_copy(row).wait_send()

    def chain_left(slot, carry):
        for route, (taken, _) in enumerate(routes):
            @pl.when(taken)
            def _():
                chain_copy(route, act, slot).wait_send()
        return carry

    lax.fori_loop(0, 2 * ny, chain_left, 0)

    def inv_left(index, carry):
        for route, (taken, _) in enumerate(routes):
            @pl.when(taken)
            def _():
                inv_copy(route, False, index).wait_send()
        return carry

    lax.fori_loop(0, pieces, inv_left, 0)

    @pl.when(is_grad)
    def _():
        cross_copy.wait_send()

    for slot in range(3):
        pltpu.make_async_copy(part.at[0], landed.at[slot], out_recv.at[slot]).wait()
        out_ref[:, slot * UNIT:(slot + 1) * UNIT] = landed[slot].astype(F32) * (1.0 / tokens)

    @pl.when(is_grad)
    def _():
        for unit in range(4):
            target, _ = out_place(unit)

            @pl.when(target != owner)
            def _():
                out_copy(unit).wait_send()


def per_device(features):
    dp_size = lax.axis_size("dp")
    owner_size = lax.axis_size("owner")
    ny, nz = dp_size // 2, owner_size // 4
    rows = features.shape[0]
    quarter = rows // 4
    pieces = 8
    blocks = BLK // UNIT
    square = (BLK, BLK)
    dma = pltpu.SemaphoreType.DMA
    return pl.pallas_call(
        functools.partial(kernel, ny, nz, rows * dp_size),
        out_shape=(
            jax.ShapeDtypeStruct((1, BLK // dp_size, BLK), F32),
            jax.ShapeDtypeStruct((BLK // 2, 3 * UNIT), F32),
        ),
        in_specs=[pl.BlockSpec(memory_space=pltpu.VMEM)],
        out_specs=[pl.BlockSpec(memory_space=pltpu.VMEM)] * 2,
        scratch_shapes=[
            pltpu.VMEM((4 * ny, quarter, BLK), BF16),
            pltpu.VMEM((4 * ny, quarter, BLK), BF16),
            pltpu.VMEM(square, F32),
            pltpu.VMEM(square, BF16),
            pltpu.VMEM(square, BF16),
            pltpu.VMEM(square, F32),
            pltpu.VMEM(square, BF16),
            pltpu.VMEM(square, BF16),
            pltpu.VMEM(square, F32),
            pltpu.VMEM(square, F32),
            pltpu.VMEM((BLK // dp_size + BLK // 2, BLK), F32),
            pltpu.VMEM(square, BF16),
            pltpu.VMEM((pieces, BLK // 2 // pieces, BLK), BF16),
            pltpu.VMEM((4, BLK // 2, UNIT), BF16),
            pltpu.VMEM((3, BLK // 2, UNIT), BF16),
            dma((2, 2 * (ny - 1))),
            dma((2, 2 * (ny - 1))),
            dma((4, 2 * ny)),
            dma((2 * ny,)),
            dma((blocks + 1,)),
            dma((blocks + 1,)),
            dma((4, pieces)),
            dma((pieces,)),
            dma((4,)),
            dma((3,)),
        ],
        compiler_params=pltpu.CompilerParams(
            collective_id=0, has_side_effects=True, vmem_limit_bytes=48 * 2**20
        ),
    )(features)


def solution(mesh):
    return jax.shard_map(
        per_device,
        mesh=mesh,
        in_specs=(P("dp", "owner"),),
        out_specs=(P("owner", "dp", None), P("dp", "owner")),
        check_vma=False,
    )
```
